32 devices in a mesh: rows: 8 (over y, x, core), aux: 4 (over z).
Axes of the slice: x: 2, y: 2, z: 4, core: 2. Of those that a mesh axis runs over, the one named last changes fastest.
Arguments:
- pair_green_block: bfloat16 [65536, 2048], P('rows', 'aux'), may hold values from -6 to 6
- cholesky_factors: bfloat16 [65536, 512], P('rows', 'aux'), may hold values from -0.09375 to 0.09375
- green_one: float32 [256, 256], replicated, may hold values from -0.375 to 0.375
- screening: float32 [512], replicated, may hold values from 0.25 to 4
Outputs:
- section_slope: float32 [65536, 2048], P('rows', 'aux')
- collision: float32 [65536], P(('rows', 'aux'))
The draws below stay inside these ranges and needn't reach their ends.
All inputs are finite; a program needn't handle non-finite values.
Results may differ from the reference program's by a relative error of at most 0.0029.
Values may be sent and summed in bfloat16 or wider, within the bound.
No kernel may reach another device: no remote copies, remote signals or barrier semaphores. Data moves between devices by JAX's collectives and lax.ppermute only.
A program may use at most 128 MiB of HBM per device.

```python
import math
import jax
import jax.numpy as jnp
from jax import lax

NORB = 256
NAUX = 512
KSLAB = 8
PAIRS = 65536
SLAB = 2048


def level_of(stream_key, dims, split, low, largest):
    gain, own = 1.0, jax.random.fold_in(stream_key, 6)
    for dim, shards_of in split:
        draws = jnp.exp(jax.random.uniform(jax.random.fold_in(own, dim), (shards_of,), jnp.float32, low / len(split), largest / len(split)))
        gain = gain * jnp.repeat(draws, dims[dim] // shards_of).reshape([-1 if axis == dim else 1 for axis in range(len(dims))])
    return gain


def normal_values(own_key, extent, scale, most, cuts=(), kind=jnp.bfloat16):
    result = scale * jax.random.normal(own_key, extent, jnp.float32)
    if cuts:
        result = result * level_of(own_key, extent, cuts, -0.22, 0.18)
    return jnp.clip(result, -most, most).astype(kind)


def setup_inputs(seed: int = 0) -> dict:
    splits = jax.random.split(jax.random.key(seed), 5)
    pair_green_block = normal_values(splits[0], (PAIRS, SLAB), 1.0, 6.0, ((0, 8), (1, 4)))
    cholesky_factors = normal_values(splits[1], (PAIRS, NAUX), (NORB * NAUX // 32) ** -0.5, 0.09375, ((0, 8), (1, 4)))
    green_one = normal_values(splits[2], (NORB, NORB), NORB ** -0.5, 0.375, (), jnp.float32)
    screening = jnp.clip(jnp.exp(jax.random.uniform(splits[3], (NAUX,), jnp.float32, math.log(0.25), math.log(4.0))), 0.25, 4.0)
    return dict(pair_green_block=pair_green_block, cholesky_factors=cholesky_factors, green_one=green_one, screening=screening)


def reference(pair_green_block, cholesky_factors, green_one, screening):
    highest = lax.Precision.HIGHEST
    projected = lax.dot_general(cholesky_factors, pair_green_block, (((0,), (0,)), ((), ())), preferred_element_type=jnp.float32)
    shaped = projected.reshape(NAUX, KSLAB, NORB)
    dressed = jnp.einsum("qkm,ml->qkl", shaped, green_one, precision=highest)
    dressed = (dressed * screening[:, None, None]).reshape(NAUX, KSLAB * NORB).astype(jnp.bfloat16)
    section_slope = jnp.dot(cholesky_factors, dressed, preferred_element_type=jnp.float32)
    trace_weights = green_one[:, :KSLAB].T.reshape(KSLAB * NORB)
    collision = jnp.dot(section_slope, trace_weights, precision=highest, preferred_element_type=jnp.float32)
    return section_slope, collision
```

```python
import functools

import jax
import jax.numpy as jnp
from jax import lax
from jax.experimental import pallas as pl
from jax.experimental.pallas import tpu as pltpu
from jax.sharding import PartitionSpec as P

HIGHEST = lax.Precision.HIGHEST
PIECES = 2


def ring_next(block, axis):
    count = lax.axis_size(axis)
    return lax.ppermute(block, axis, [(i, (i + 1) % count) for i in range(count)])


def sum_over(block, axis, bits):
    count = lax.axis_size(axis)
    for bit in bits:
        block = block + lax.ppermute(block, axis, [(i, i ^ bit) for i in range(count)])
    return block


def sum_over_rows(block):
    count = lax.axis_size("rows")
    if count & (count - 1):
        return lax.psum(block, "rows")
    bits = [1 << b for b in range(count.bit_length() - 1)]
    block = sum_over(block, "rows", bits[:1])
    rest = bits[1:]
    half = block.shape[0] // 2
    return jnp.concatenate(
        [sum_over(block[:half], "rows", rest), sum_over(block[half:], "rows", rest[::-1])], axis=0
    )


def project(piece, green_rows):
    return lax.dot_general(
        piece, green_rows, (((0,), (0,)), ((), ())), preferred_element_type=jnp.float32
    )


def slope_body(shards, pieces, blocks, *refs):
    dressed_ref, out_ref = refs[shards * pieces], refs[shards * pieces + 1]
    here = pl.program_id(0) // blocks
    for i in range(pieces):

        @pl.when(here == i)
        def _():
            basis = jnp.concatenate([refs[s * pieces + i][...] for s in range(shards)], axis=1)
            out_ref[...] = jnp.dot(basis, dressed_ref[...], preferred_element_type=jnp.float32)


def slope(steps, dressed):
    pieces = len(steps[0])
    length, vectors = steps[0][0].shape
    depth, columns = dressed.shape
    block = min(length, 1024)
    blocks = length // block
    factor_specs = [
        pl.BlockSpec((block, vectors), lambda g, i=i: (jnp.clip(g - i * blocks, 0, blocks - 1), 0))
        for _ in steps
        for i in range(pieces)
    ]
    rows = pieces * length
    return pl.pallas_call(
        functools.partial(slope_body, len(steps), pieces, blocks),
        grid=(pieces * blocks,),
        out_shape=jax.ShapeDtypeStruct((rows, columns), jnp.float32),
        in_specs=factor_specs + [pl.BlockSpec((depth, columns), lambda g: (0, 0))],
        out_specs=pl.BlockSpec((block, columns), lambda g: (g, 0)),
        compiler_params=pltpu.CompilerParams(vmem_limit_bytes=48 * 1024 * 1024),
        cost_estimate=pl.CostEstimate(
            flops=2 * rows * depth * columns,
            bytes_accessed=rows * depth * 2 + rows * columns * 4,
            transcendentals=0,
        ),
    )(*[piece for step in steps for piece in step], dressed)


def local(pair_green_block, cholesky_factors, green_one, screening):
    rows, columns = pair_green_block.shape
    vectors = cholesky_factors.shape[1]
    norb = green_one.shape[0]
    orb_count = columns // norb
    aux_size = lax.axis_size("aux")
    me = lax.axis_index("aux")
    owners = [lax.rem(me - step + aux_size, aux_size) for step in range(aux_size)]

    length = rows // PIECES
    pieces = [
        lax.slice_in_dim(cholesky_factors, i * length, (i + 1) * length, axis=0)
        for i in range(PIECES)
    ]
    steps = [pieces]
    for _ in range(1, aux_size):
        steps.append([ring_next(piece, "aux") for piece in steps[-1]])

    first_orb = me * orb_count
    trace_weights = lax.dynamic_slice_in_dim(green_one, first_orb, orb_count, 1).T.reshape(columns)

    dressed, traced = [], []
    for step, own_pieces in enumerate(steps):
        projection = sum(
            project(piece, pair_green_block[i * length : (i + 1) * length])
            for i, piece in enumerate(own_pieces)
        )
        projection = sum_over_rows(projection)
        weights = lax.dynamic_slice_in_dim(screening, owners[step] * vectors, vectors, 0)
        mixed = jnp.concatenate(
            [
                jnp.dot(projection[:, k * norb : (k + 1) * norb], green_one, precision=HIGHEST)
                for k in range(orb_count)
            ],
            axis=1,
        )
        dressed.append((mixed * weights[:, None]).astype(jnp.bfloat16))
        traced.append(jnp.sum(dressed[-1].astype(jnp.float32) * trace_weights[None, :], axis=1))

    section_slope = slope(steps, jnp.concatenate(dressed, axis=0))

    trace = jnp.zeros((aux_size, vectors), jnp.float32)
    for step in range(aux_size):
        trace = lax.dynamic_update_slice_in_dim(trace, traced[step][None], owners[step], 0)
    total = trace
    for shift in range(1, aux_size):
        total = total + lax.ppermute(
            trace, "aux", [(i, (i + shift) % aux_size) for i in range(aux_size)]
        )
    share = rows // aux_size
    collision = jnp.zeros((share,), jnp.float32)
    for step in range(aux_size):
        mine = lax.select_n(
            me * share >= length,
            *[lax.dynamic_slice_in_dim(piece, lax.rem(me * share, length), share, 0) for piece in steps[step]]
        ).astype(jnp.float32)
        vec = lax.dynamic_slice_in_dim(total, owners[step], 1, 0)[0]
        collision = collision + jnp.dot(mine, vec, precision=HIGHEST)
    return section_slope, collision


def solution(mesh):
    placed = (P("rows", "aux"), P("rows", "aux"), P(), P())
    return jax.shard_map(
        local,
        mesh=mesh,
        in_specs=placed,
        out_specs=(P("rows", "aux"), P(("rows", "aux"))),
        check_vma=False,
    )
```

```python
import functools

import jax
import jax.numpy as jnp
from jax import lax
from jax.experimental import pallas as pl
from jax.experimental.pallas import tpu as pltpu
from jax.sharding import PartitionSpec as P

HIGHEST = lax.Precision.HIGHEST
PIECES = 2
MIB = 1024 * 1024
FREE = pl.CostEstimate(flops=0, bytes_accessed=0, transcendentals=0)
ANYWHERE = pl.BlockSpec(memory_space=pl.ANY)


def shifted(block, axis, shift):
    count = lax.axis_size(axis)
    return lax.ppermute(block, axis, [(i, (i + shift) % count) for i in range(count)])


def exchanged(block, axis, bit):
    count = lax.axis_size(axis)
    return lax.ppermute(block, axis, [(i, i ^ bit) for i in range(count)])


def project_body(blocks, halved, *refs):
    piece_ref, green_ref, acc_ref = refs[:3]
    total_ref = refs[-1]
    at = pl.program_id(0)

    @pl.when(at == 0)
    def _():
        total_ref[...] = acc_ref[...]

    total_ref[...] += lax.dot_general(
        piece_ref[...], green_ref[...], (((0,), (0,)), ((), ())), preferred_element_type=jnp.float32
    )

    @pl.when(at == blocks - 1)
    def _():
        if halved:
            keep_ref, send_ref = refs[-3:-1]
            half = keep_ref.shape[0]
            upper = lax.rem(lax.axis_index("rows"), 2)
            keep_ref[...] = total_ref[pl.ds(upper * half, half), :]
            send_ref[...] = total_ref[pl.ds((1 - upper) * half, half), :]
        else:
            refs[-2][...] = total_ref[...]


def project(piece, green, first, so_far, halved, after):
    length, vectors = piece.shape
    columns = green.shape[1]
    block = min(length, 1024)
    blocks = length // block
    start = first // block
    whole = pl.BlockSpec((vectors, columns), lambda i: (0, 0))
    part = pl.BlockSpec((vectors // 2, columns), lambda i: (0, 0))
    return pl.pallas_call(
        functools.partial(project_body, blocks, halved),
        grid=(blocks,),
        out_shape=[jax.ShapeDtypeStruct((vectors // 2, columns), jnp.float32)] * 2
        if halved
        else jax.ShapeDtypeStruct((vectors, columns), jnp.float32),
        in_specs=[
            pl.BlockSpec((block, vectors), lambda i: (i, 0)),
            pl.BlockSpec((block, columns), lambda i: (i + start, 0)),
            whole,
        ]
        + [ANYWHERE] * len(after),
        out_specs=[part] * 2 if halved else whole,
        scratch_shapes=[pltpu.VMEM((vectors, columns), jnp.float32)],
        compiler_params=pltpu.CompilerParams(vmem_limit_bytes=12 * MIB),
        cost_estimate=FREE,
    )(piece, green, so_far, *after)


def dress_body(step, mine_ref, other_ref, weights_ref, green_ref, dressed_ref):
    half = mine_ref.shape[0]
    norb = green_ref.shape[0]
    aux_size = lax.axis_size("aux")
    owner = lax.rem(lax.axis_index("aux") - step + aux_size, aux_size)
    upper = lax.rem(lax.axis_index("rows"), 2)
    weights = weights_ref[pl.ds((owner * 2 + upper) * half, half), :]
    total = mine_ref[...] + other_ref[...]
    green = green_ref[...]
    for first in range(0, total.shape[1], norb):
        mixed = jnp.dot(
            total[:, first : first + norb],
            green,
            precision=HIGHEST,
            preferred_element_type=jnp.float32,
        )
        dressed_ref[:, first : first + norb] = (mixed * weights).astype(jnp.bfloat16)


def dress(step, mine, other, weights, green_one):
    return pl.pallas_call(
        functools.partial(dress_body, step),
        out_shape=jax.ShapeDtypeStruct(mine.shape, jnp.bfloat16),
        cost_estimate=FREE,
    )(mine, other, weights, green_one)


def join_body(mine_ref, other_ref, trace_ref, dressed_ref, traced_ref):
    half = mine_ref.shape[0]
    upper = lax.rem(lax.axis_index("rows"), 2)
    dressed_ref[pl.ds(pl.multiple_of(upper * half, half), half), :] = mine_ref[...]
    dressed_ref[pl.ds(pl.multiple_of((1 - upper) * half, half), half), :] = other_ref[...]
    traced_ref[...] = lax.dot_general(
        trace_ref[...],
        dressed_ref[...].astype(jnp.float32),
        (((1,), (1,)), ((), ())),
        precision=HIGHEST,
        preferred_element_type=jnp.float32,
    )


def join(mine, other, trace_weights):
    half, columns = mine.shape
    return pl.pallas_call(
        join_body,
        out_shape=[
            jax.ShapeDtypeStruct((2 * half, columns), jnp.bfloat16),
            jax.ShapeDtypeStruct((1, 2 * half), jnp.float32),
        ],
        cost_estimate=FREE,
    )(mine, other, trace_weights)


def sum_and_dress(step, keep, send, weights, green_one, trace_weights):
    count = lax.axis_size("rows")
    total, other = keep, exchanged(send, "rows", 1)
    bit = 2
    while bit < count:
        total = total + other
        other = exchanged(total, "rows", bit)
        bit *= 2
    mine = dress(step, total, other, weights, green_one)
    return join(mine, exchanged(mine, "rows", 1), trace_weights)


def slope_body(shards, pieces, blocks, *refs):
    dressed_refs, out_ref = refs[shards * pieces : -1], refs[-1]
    here = pl.program_id(0) // blocks
    dressed = jnp.concatenate([ref[...] for ref in dressed_refs], axis=0)
    for i in range(pieces):

        @pl.when(here == i)
        def _():
            basis = jnp.concatenate([refs[s * pieces + i][...] for s in range(shards)], axis=1)
            out_ref[...] = jnp.dot(basis, dressed, preferred_element_type=jnp.float32)


def slope(steps, dressed):
    pieces = len(steps[0])
    length, vectors = steps[0][0].shape
    columns = dressed[0].shape[1]
    depth = len(steps) * vectors
    block = min(length, 512)
    blocks = length // block
    factor_specs = [
        pl.BlockSpec((block, vectors), lambda g, i=i: (jnp.clip(g - i * blocks, 0, blocks - 1), 0))
        for _ in steps
        for i in range(pieces)
    ]
    rows = pieces * length
    return pl.pallas_call(
        functools.partial(slope_body, len(steps), pieces, blocks),
        grid=(pieces * blocks,),
        out_shape=jax.ShapeDtypeStruct((rows, columns), jnp.float32),
        in_specs=factor_specs + [pl.BlockSpec((vectors, columns), lambda g: (0, 0))] * len(steps),
        out_specs=pl.BlockSpec((block, columns), lambda g: (g, 0)),
        compiler_params=pltpu.CompilerParams(vmem_limit_bytes=16 * MIB),
        cost_estimate=pl.CostEstimate(
            flops=2 * rows * depth * columns,
            bytes_accessed=rows * depth * 2 + rows * columns * 4,
            transcendentals=0,
        ),
    )(*[piece for step in steps for piece in step], *dressed)


def collide_body(shards, pieces, per_piece, me_ref, *refs):
    trace_refs, out_ref = refs[shards * pieces : -1], refs[-1]
    trace = trace_refs[0][...]
    for shift in range(1, shards):
        came = trace_refs[shift][...]
        trace = trace + jnp.concatenate([came[shards - shift :], came[: shards - shift]], axis=0)
    here = me_ref[0] // per_piece
    for i in range(pieces):

        @pl.when(here == i)
        def _():
            total = jnp.zeros(out_ref.shape, jnp.float32)
            for s in range(shards):
                row = trace[s : s + 1]
                high = row.astype(jnp.bfloat16)
                rest = row - high.astype(jnp.float32)
                middle = rest.astype(jnp.bfloat16)
                low = (rest - middle.astype(jnp.float32)).astype(jnp.bfloat16)
                for part in (low, middle, high):
                    total += lax.dot_general(
                        part,
                        refs[s * pieces + i][...],
                        (((1,), (1,)), ((), ())),
                        preferred_element_type=jnp.float32,
                    )
            out_ref[...] = total


def collide(steps, traces):
    shards, pieces = len(steps), len(steps[0])
    length, vectors = steps[0][0].shape
    per_piece = shards // pieces
    share = length // per_piece
    return pl.pallas_call(
        functools.partial(collide_body, shards, pieces, per_piece),
        grid_spec=pltpu.PrefetchScalarGridSpec(
            num_scalar_prefetch=1,
            grid=(1,),
            in_specs=[
                pl.BlockSpec(
                    (share, vectors),
                    lambda g, me, i=i: (jnp.clip(me[0] - i * per_piece, 0, per_piece - 1), 0),
                )
                for _ in steps
                for i in range(pieces)
            ]
            + [pl.BlockSpec((shards, vectors), lambda g, me: (0, 0))] * shards,
            out_specs=pl.BlockSpec((1, share), lambda g, me: (0, 0)),
        ),
        out_shape=jax.ShapeDtypeStruct((1, share), jnp.float32),
        compiler_params=pltpu.CompilerParams(vmem_limit_bytes=16 * MIB),
        cost_estimate=FREE,
    )(
        lax.axis_index("aux").astype(jnp.int32)[None],
        *[piece for step in steps for piece in step],
        *traces,
    )[0]


def local(pair_green_block, cholesky_factors, green_one, screening):
    rows, columns = pair_green_block.shape
    vectors = cholesky_factors.shape[1]
    norb = green_one.shape[0]
    orb_count = columns // norb
    aux_size = lax.axis_size("aux")
    me = lax.axis_index("aux")
    length = rows // PIECES

    trace_weights = lax.dynamic_slice_in_dim(
        green_one, me * orb_count, orb_count, 1
    ).T.reshape(1, columns)
    weights = screening[:, None]
    zeros = jnp.zeros((vectors, columns), jnp.float32)

    steps, dressed, traced = [], [], []
    for step in range(aux_size):
        if step == 0:
            pieces = [
                lax.slice_in_dim(cholesky_factors, i * length, (i + 1) * length, axis=0)
                for i in range(PIECES)
            ]
        else:
            pieces = [shifted(piece, "aux", 1) for piece in steps[-1]]
        steps.append(pieces)
        so_far = zeros
        for i, piece in enumerate(pieces):
            so_far = project(
                piece, pair_green_block, i * length, so_far, i == PIECES - 1,
                dressed[-1:] + traced[-1:],
            )
        both, trace = sum_and_dress(step, *so_far, weights, green_one, trace_weights)
        dressed.append(both)
        traced.append(trace)

    trace = jnp.concatenate(traced, axis=0)
    traces = [trace] + [shifted(trace, "aux", shift) for shift in range(1, aux_size)]
    section_slope = slope(steps, dressed)
    return section_slope, collide(steps, traces)


def solution(mesh):
    placed = (P("rows", "aux"), P("rows", "aux"), P(), P())
    return jax.shard_map(
        local,
        mesh=mesh,
        in_specs=placed,
        out_specs=(P("rows", "aux"), P(("rows", "aux"))),
        check_vma=False,
    )
```

```python
import functools

import jax
import jax.numpy as jnp
from jax import lax
from jax.experimental import pallas as pl
from jax.experimental.pallas import tpu as pltpu
from jax.sharding import PartitionSpec as P

HIGHEST = lax.Precision.HIGHEST
PIECES = 2
MIB = 1024 * 1024
FREE = pl.CostEstimate(flops=0, bytes_accessed=0, transcendentals=0)
ANYWHERE = pl.BlockSpec(memory_space=pl.ANY)


def shifted(block, axis, shift):
    count = lax.axis_size(axis)
    return lax.ppermute(block, axis, [(i, (i + shift) % count) for i in range(count)])


def exchanged(block, axis, bit):
    count = lax.axis_size(axis)
    return lax.ppermute(block, axis, [(i, i ^ bit) for i in range(count)])


def gate_body(*refs):
    del refs


def gate(block, *after):
    return pl.pallas_call(
        gate_body,
        out_shape=jax.ShapeDtypeStruct(block.shape, block.dtype),
        in_specs=[ANYWHERE] * (1 + len(after)),
        out_specs=ANYWHERE,
        input_output_aliases={0: 0},
        cost_estimate=FREE,
    )(block, *after)


def project_body(first, block, piece_ref, green_ref, acc_ref, total_ref):
    total_ref[...] = acc_ref[...]

    def step(piece, green):
        total_ref[...] += lax.dot_general(
            piece[...], green[...], (((0,), (0,)), ((), ())), preferred_element_type=jnp.float32
        )

    length, vectors = piece_ref.shape
    columns = green_ref.shape[1]
    pltpu.emit_pipeline(
        step,
        grid=(length // block,),
        in_specs=[
            pl.BlockSpec((block, vectors), lambda i: (i, 0)),
            pl.BlockSpec((block, columns), lambda i: (i + first // block, 0)),
        ],
    )(piece_ref, green_ref)


def project(piece, green, first, so_far):
    length, vectors = piece.shape
    columns = green.shape[1]
    in_vmem = pl.BlockSpec(memory_space=pltpu.VMEM)
    return pl.pallas_call(
        functools.partial(project_body, first, min(length, 1024)),
        out_shape=jax.ShapeDtypeStruct((vectors, columns), jnp.float32),
        in_specs=[ANYWHERE, pl.BlockSpec(memory_space=pltpu.HBM), in_vmem],
        out_specs=in_vmem,
        compiler_params=pltpu.CompilerParams(vmem_limit_bytes=12 * MIB),
        cost_estimate=FREE,
    )(piece, green, so_far)


def project_plain(piece, green_rows):
    return lax.dot_general(
        piece, green_rows, (((0,), (0,)), ((), ())), preferred_element_type=jnp.float32
    )


def dress(projection, weights, green_one, trace_weights):
    norb = green_one.shape[0]
    mixed = jnp.concatenate(
        [
            jnp.dot(projection[:, first : first + norb], green_one, precision=HIGHEST)
            for first in range(0, projection.shape[1], norb)
        ],
        axis=1,
    )
    rounded = lax.reduce_precision(mixed * weights[:, None], 8, 7)
    traced = lax.dot_general(
        trace_weights, rounded, (((1,), (1,)), ((), ())), precision=HIGHEST
    )
    return rounded.astype(jnp.bfloat16), traced


def dress_kernel_body(step, mine_ref, other_ref, weights_ref, green_ref, dressed_ref):
    half = mine_ref.shape[0]
    norb = green_ref.shape[0]
    aux_size = lax.axis_size("aux")
    owner = lax.rem(lax.axis_index("aux") - step + aux_size, aux_size)
    upper = lax.rem(lax.axis_index("rows"), 2)
    weights = weights_ref[pl.ds((owner * 2 + upper) * half, half), :]
    total = mine_ref[...] + other_ref[...]
    green = green_ref[...]
    for first in range(0, total.shape[1], norb):
        mixed = jnp.dot(
            total[:, first : first + norb],
            green,
            precision=HIGHEST,
            preferred_element_type=jnp.float32,
        )
        dressed_ref[:, first : first + norb] = (mixed * weights).astype(jnp.bfloat16)


def dress_kernel(step, mine, other, weights, green_one):
    return pl.pallas_call(
        functools.partial(dress_kernel_body, step),
        out_shape=jax.ShapeDtypeStruct(mine.shape, jnp.bfloat16),
        cost_estimate=FREE,
    )(mine, other, weights, green_one)


def join_kernel_body(mine_ref, other_ref, trace_ref, dressed_ref, traced_ref):
    half = mine_ref.shape[0]
    upper = lax.rem(lax.axis_index("rows"), 2)
    dressed_ref[pl.ds(pl.multiple_of(upper * half, half), half), :] = mine_ref[...]
    dressed_ref[pl.ds(pl.multiple_of((1 - upper) * half, half), half), :] = other_ref[...]
    row = trace_ref[...]
    high = row.astype(jnp.bfloat16).astype(jnp.float32)
    middle = (row - high).astype(jnp.bfloat16).astype(jnp.float32)
    parts = jnp.concatenate(
        [row - high - middle, middle, high, jnp.zeros((5, row.shape[1]), jnp.float32)], axis=0
    )
    traced = lax.dot_general(
        parts.astype(jnp.bfloat16),
        dressed_ref[...],
        (((1,), (1,)), ((), ())),
        preferred_element_type=jnp.float32,
    )
    traced_ref[...] = jnp.sum(traced, axis=0, keepdims=True)


def join_kernel(mine, other, trace_weights):
    half, columns = mine.shape
    return pl.pallas_call(
        join_kernel_body,
        out_shape=[
            jax.ShapeDtypeStruct((2 * half, columns), jnp.bfloat16),
            jax.ShapeDtypeStruct((1, 2 * half), jnp.float32),
        ],
        cost_estimate=FREE,
    )(mine, other, trace_weights)


def sum_and_dress(step, projection, weights, green_one, trace_weights):
    count, aux_size = lax.axis_size("rows"), lax.axis_size("aux")
    half = projection.shape[0] // 2
    upper = lax.rem(lax.axis_index("rows"), 2) == 1
    low, high = projection[:half], projection[half:]
    total = jnp.where(upper, high, low)
    other = exchanged(jnp.where(upper, low, high), "rows", 1)
    bit = 2
    while bit < count:
        total = total + other
        other = exchanged(total, "rows", bit)
        bit *= 2
    if step < aux_size - 1:
        mine = dress_kernel(step, total, other, weights[:, None], green_one)
        return join_kernel(mine, exchanged(mine, "rows", 1), trace_weights)
    owner = lax.rem(lax.axis_index("aux") - step + aux_size, aux_size)
    first = (2 * owner + lax.rem(lax.axis_index("rows"), 2)) * half
    mine, mine_traced = dress(
        total + other,
        lax.dynamic_slice_in_dim(weights, first, half, 0),
        green_one,
        trace_weights,
    )
    other = exchanged(mine, "rows", 1)
    other_traced = exchanged(mine_traced, "rows", 1)
    dressed = jnp.concatenate(
        [jnp.where(upper, other, mine), jnp.where(upper, mine, other)], axis=0
    )
    traced = jnp.concatenate(
        [jnp.where(upper, other_traced, mine_traced), jnp.where(upper, mine_traced, other_traced)],
        axis=1,
    )
    return dressed, traced


def slope_body(shards, pieces, blocks, share_blocks, me_ref, *refs):
    factor_refs = refs[: shards * pieces]
    dressed_refs = refs[shards * pieces : shards * pieces + shards]
    trace_refs = refs[shards * pieces + shards : -3]
    slope_ref, collision_ref, trace_ref = refs[-3:]
    at = pl.program_id(0)

    @pl.when(at == 0)
    def _():
        trace = trace_refs[0][...]
        for shift in range(1, shards):
            came = trace_refs[shift][...]
            trace = trace + jnp.concatenate(
                [came[shards - shift :], came[: shards - shift]], axis=0
            )
        row = jnp.concatenate([trace[s : s + 1] for s in range(shards)], axis=1)
        high = row.astype(jnp.bfloat16).astype(jnp.float32)
        middle = (row - high).astype(jnp.bfloat16).astype(jnp.float32)
        low = row - high - middle
        trace_ref[...] = jnp.concatenate(
            [low, middle, high, jnp.zeros((5, row.shape[1]), jnp.float32)], axis=0
        ).astype(jnp.bfloat16)

    dressed = jnp.concatenate([ref[...] for ref in dressed_refs], axis=0)
    first = me_ref[0] * share_blocks
    for i in range(pieces):

        @pl.when(at // blocks == i)
        def _():
            basis = jnp.concatenate(
                [factor_refs[s * pieces + i][...] for s in range(shards)], axis=1
            )
            slope_ref[...] = jnp.dot(basis, dressed, preferred_element_type=jnp.float32)

            @pl.when((at >= first) & (at < first + share_blocks))
            def _():
                parts = lax.dot_general(
                    trace_ref[...],
                    basis,
                    (((1,), (1,)), ((), ())),
                    preferred_element_type=jnp.float32,
                )
                collision_ref[pl.ds(at - first, 1), :] = jnp.sum(parts, axis=0, keepdims=True)


def slope(steps, dressed, traces):
    shards, pieces = len(steps), len(steps[0])
    length, vectors = steps[0][0].shape
    columns = dressed[0].shape[1]
    depth = shards * vectors
    rows = pieces * length
    share = rows // shards
    block = min(length, share, 1024)
    blocks = length // block
    factor_specs = [
        pl.BlockSpec(
            (block, vectors), lambda g, me, i=i: (jnp.clip(g - i * blocks, 0, blocks - 1), 0)
        )
        for _ in steps
        for i in range(pieces)
    ]
    whole = lambda g, me: (0, 0)
    slopes, collision = pl.pallas_call(
        functools.partial(slope_body, shards, pieces, blocks, share // block),
        grid_spec=pltpu.PrefetchScalarGridSpec(
            num_scalar_prefetch=1,
            grid=(pieces * blocks,),
            in_specs=factor_specs
            + [pl.BlockSpec((vectors, columns), whole)] * shards
            + [pl.BlockSpec((shards, vectors), whole)] * shards,
            out_specs=[
                pl.BlockSpec((block, columns), lambda g, me: (g, 0)),
                pl.BlockSpec((share // block, block), whole),
            ],
            scratch_shapes=[pltpu.VMEM((8, depth), jnp.bfloat16)],
        ),
        out_shape=[
            jax.ShapeDtypeStruct((rows, columns), jnp.float32),
            jax.ShapeDtypeStruct((share // block, block), jnp.float32),
        ],
        compiler_params=pltpu.CompilerParams(vmem_limit_bytes=20 * MIB),
        cost_estimate=pl.CostEstimate(
            flops=2 * rows * depth * columns,
            bytes_accessed=rows * depth * 2 + rows * columns * 4,
            transcendentals=0,
        ),
    )(
        lax.axis_index("aux").astype(jnp.int32)[None],
        *[piece for step in steps for piece in step],
        *dressed,
        *traces,
    )
    return slopes, collision.reshape(share)


def local(pair_green_block, cholesky_factors, green_one, screening):
    rows, columns = pair_green_block.shape
    vectors = cholesky_factors.shape[1]
    norb = green_one.shape[0]
    orb_count = columns // norb
    aux_size = lax.axis_size("aux")
    me = lax.axis_index("aux")
    length = rows // PIECES

    trace_weights = lax.dynamic_slice_in_dim(
        green_one, me * orb_count, orb_count, 1
    ).T.reshape(1, columns)
    steps, dressed, traced = [], [], []
    for step in range(aux_size):
        total = jnp.zeros((vectors, columns), jnp.float32)
        pieces = []
        for i in range(PIECES):
            green = (pair_green_block, i * length)
            if step == 0:
                piece = lax.slice_in_dim(cholesky_factors, i * length, (i + 1) * length, axis=0)
            elif i == 0:
                piece = gate(shifted(steps[-1][i], "aux", 1), dressed[-1], traced[-1])
            else:
                piece = gate(shifted(steps[-1][i], "aux", 1), total)
            pieces.append(piece)
            if step < aux_size - 1:
                total = project(piece, pair_green_block, i * length, total)
            else:
                total = total + project_plain(
                    piece, pair_green_block[i * length : (i + 1) * length]
                )
        steps.append(pieces)
        both, trace = sum_and_dress(step, total, screening, green_one, trace_weights)
        dressed.append(both)
        traced.append(trace)

    trace = jnp.concatenate(traced, axis=0)
    traces = [trace] + [shifted(trace, "aux", shift) for shift in range(1, aux_size)]
    return slope(steps, dressed, traces)


def solution(mesh):
    placed = (P("rows", "aux"), P("rows", "aux"), P(), P())
    return jax.shard_map(
        local,
        mesh=mesh,
        in_specs=placed,
        out_specs=(P("rows", "aux"), P(("rows", "aux"))),
        check_vma=False,
    )
```

```python
import functools

import jax
import jax.numpy as jnp
from jax import lax
from jax.experimental import pallas as pl
from jax.experimental.pallas import tpu as pltpu
from jax.sharding import PartitionSpec as P

HIGHEST = lax.Precision.HIGHEST
PIECES = 2
MIB = 1024 * 1024
FREE = pl.CostEstimate(flops=0, bytes_accessed=0, transcendentals=0)
ANYWHERE = pl.BlockSpec(memory_space=pl.ANY)
IN_VMEM = pl.BlockSpec(memory_space=pltpu.VMEM)


vmem_shape = pltpu.VMEM


def in_vmem(block):
    return pltpu.with_memory_space_constraint(block, pltpu.VMEM)


def in_hbm(block):
    return pltpu.with_memory_space_constraint(block, pltpu.HBM)


def shifted(block, axis, shift):
    count = lax.axis_size(axis)
    return lax.ppermute(block, axis, [(i, (i + shift) % count) for i in range(count)])


def exchanged(block, axis, bit):
    count = lax.axis_size(axis)
    return lax.ppermute(block, axis, [(i, i ^ bit) for i in range(count)])


def gate_body(*refs):
    del refs


def gate(block, *after):
    return pl.pallas_call(
        gate_body,
        out_shape=jax.ShapeDtypeStruct(block.shape, block.dtype),
        in_specs=[ANYWHERE] * (1 + len(after)),
        out_specs=ANYWHERE,
        input_output_aliases={0: 0},
        compiler_params=pltpu.CompilerParams(vmem_limit_bytes=2 * MIB),
        cost_estimate=FREE,
    )(in_vmem(block), *after)


def load_body(count, *refs):
    arrays, copies, semaphores = refs[:count], refs[count : 2 * count], refs[-1]
    moves = [
        pltpu.make_async_copy(array, copy, semaphores.at[i])
        for i, (array, copy) in enumerate(zip(arrays, copies))
    ]
    for move in moves:
        move.start()
    for move in moves:
        move.wait()


def load(*arrays):
    return pl.pallas_call(
        functools.partial(load_body, len(arrays)),
        out_shape=[vmem_shape(array.shape, array.dtype) for array in arrays],
        in_specs=[pl.BlockSpec(memory_space=pltpu.HBM)] * len(arrays),
        out_specs=[IN_VMEM] * len(arrays),
        scratch_shapes=[pltpu.SemaphoreType.DMA((len(arrays),))],
        compiler_params=pltpu.CompilerParams(vmem_limit_bytes=2 * MIB),
        cost_estimate=FREE,
    )(*[in_hbm(array) for array in arrays])


def project_body(first, block, piece_ref, green_ref, acc_ref, total_ref):
    total_ref[...] = acc_ref[...]

    @pl.loop(0, piece_ref.shape[0] // block)
    def _(i):
        at = pl.multiple_of(i * block, block)
        total_ref[...] += lax.dot_general(
            piece_ref[pl.ds(at, block), :],
            green_ref[pl.ds(first + at, block), :],
            (((0,), (0,)), ((), ())),
            preferred_element_type=jnp.float32,
        )


def project(piece, green, first, so_far):
    length, vectors = piece.shape
    columns = green.shape[1]
    return pl.pallas_call(
        functools.partial(project_body, first, min(length, 1024)),
        out_shape=jax.ShapeDtypeStruct((vectors, columns), jnp.float32),
        in_specs=[IN_VMEM] * 3,
        out_specs=IN_VMEM,
        compiler_params=pltpu.CompilerParams(vmem_limit_bytes=6 * MIB),
        cost_estimate=FREE,
    )(in_vmem(piece), green, so_far)


def project_plain(piece, green_rows):
    return lax.dot_general(
        piece, green_rows, (((0,), (0,)), ((), ())), preferred_element_type=jnp.float32
    )


def dress(projection, weights, green_one, trace_weights):
    norb = green_one.shape[0]
    mixed = jnp.concatenate(
        [
            jnp.dot(projection[:, first : first + norb], green_one, precision=HIGHEST)
            for first in range(0, projection.shape[1], norb)
        ],
        axis=1,
    )
    rounded = lax.reduce_precision(mixed * weights[:, None], 8, 7)
    traced = lax.dot_general(
        trace_weights, rounded, (((1,), (1,)), ((), ())), precision=HIGHEST
    )
    return rounded.astype(jnp.bfloat16), traced


def dress_kernel_body(step, mine_ref, other_ref, weights_ref, green_ref, dressed_ref):
    half = mine_ref.shape[0]
    norb = green_ref.shape[0]
    aux_size = lax.axis_size("aux")
    owner = lax.rem(lax.axis_index("aux") - step + aux_size, aux_size)
    upper = lax.rem(lax.axis_index("rows"), 2)
    weights = weights_ref[pl.ds((owner * 2 + upper) * half, half), :]
    total = mine_ref[...] + other_ref[...]
    green = green_ref[...]
    for first in range(0, total.shape[1], norb):
        mixed = jnp.dot(
            total[:, first : first + norb],
            green,
            precision=HIGHEST,
            preferred_element_type=jnp.float32,
        )
        dressed_ref[:, first : first + norb] = (mixed * weights).astype(jnp.bfloat16)


def dress_kernel(step, mine, other, weights, green_one):
    return pl.pallas_call(
        functools.partial(dress_kernel_body, step),
        out_shape=jax.ShapeDtypeStruct(mine.shape, jnp.bfloat16),
        compiler_params=pltpu.CompilerParams(vmem_limit_bytes=6 * MIB),
        cost_estimate=FREE,
    )(mine, other, weights, green_one)


def join_kernel_body(mine_ref, other_ref, trace_ref, dressed_ref, traced_ref):
    half = mine_ref.shape[0]
    upper = lax.rem(lax.axis_index("rows"), 2)
    dressed_ref[pl.ds(pl.multiple_of(upper * half, half), half), :] = mine_ref[...]
    dressed_ref[pl.ds(pl.multiple_of((1 - upper) * half, half), half), :] = other_ref[...]
    row = trace_ref[...]
    high = row.astype(jnp.bfloat16).astype(jnp.float32)
    middle = (row - high).astype(jnp.bfloat16).astype(jnp.float32)
    parts = jnp.concatenate(
        [row - high - middle, middle, high, jnp.zeros((5, row.shape[1]), jnp.float32)], axis=0
    )
    traced = lax.dot_general(
        parts.astype(jnp.bfloat16),
        dressed_ref[...],
        (((1,), (1,)), ((), ())),
        preferred_element_type=jnp.float32,
    )
    traced_ref[...] = jnp.sum(traced, axis=0, keepdims=True)


def join_kernel(mine, other, trace_weights):
    half, columns = mine.shape
    return pl.pallas_call(
        join_kernel_body,
        out_shape=[
            jax.ShapeDtypeStruct((2 * half, columns), jnp.bfloat16),
            jax.ShapeDtypeStruct((1, 2 * half), jnp.float32),
        ],
        compiler_params=pltpu.CompilerParams(vmem_limit_bytes=6 * MIB),
        cost_estimate=FREE,
    )(mine, other, trace_weights)


def sum_and_dress(step, projection, weights, green_one, trace_weights):
    count, aux_size = lax.axis_size("rows"), lax.axis_size("aux")
    half = projection.shape[0] // 2
    upper = lax.rem(lax.axis_index("rows"), 2) == 1
    low, high = projection[:half], projection[half:]
    total = jnp.where(upper, high, low)
    other = exchanged(jnp.where(upper, low, high), "rows", 1)
    bit = 2
    while bit < count:
        total = total + other
        other = exchanged(total, "rows", bit)
        bit *= 2
    if step < aux_size - 1:
        mine = dress_kernel(step, total, other, weights[:, None], green_one)
        return join_kernel(mine, exchanged(mine, "rows", 1), trace_weights)
    owner = lax.rem(lax.axis_index("aux") - step + aux_size, aux_size)
    first = (2 * owner + lax.rem(lax.axis_index("rows"), 2)) * half
    mine, mine_traced = dress(
        total + other,
        lax.dynamic_slice_in_dim(weights, first, half, 0),
        green_one,
        trace_weights,
    )
    other = exchanged(mine, "rows", 1)
    other_traced = exchanged(mine_traced, "rows", 1)
    dressed = jnp.concatenate(
        [jnp.where(upper, other, mine), jnp.where(upper, mine, other)], axis=0
    )
    traced = jnp.concatenate(
        [jnp.where(upper, other_traced, mine_traced), jnp.where(upper, mine_traced, other_traced)],
        axis=1,
    )
    return dressed, traced


def slope_body(shards, pieces, block, share_blocks, me_ref, *refs):
    factor_refs = refs[: shards * pieces]
    dressed_refs = refs[shards * pieces : shards * pieces + shards]
    trace_refs = refs[shards * pieces + shards : -3]
    slope_ref, collision_ref, trace_ref = refs[-3:]
    at = pl.program_id(0)
    blocks = factor_refs[0].shape[0] // block

    @pl.when(at == 0)
    def _():
        trace = trace_refs[0][...]
        for shift in range(1, shards):
            came = trace_refs[shift][...]
            trace = trace + jnp.concatenate(
                [came[shards - shift :], came[: shards - shift]], axis=0
            )
        row = jnp.concatenate([trace[s : s + 1] for s in range(shards)], axis=1)
        high = row.astype(jnp.bfloat16).astype(jnp.float32)
        middle = (row - high).astype(jnp.bfloat16).astype(jnp.float32)
        low = row - high - middle
        trace_ref[...] = jnp.concatenate(
            [low, middle, high, jnp.zeros((5, row.shape[1]), jnp.float32)], axis=0
        ).astype(jnp.bfloat16)

    dressed = jnp.concatenate([ref[...] for ref in dressed_refs], axis=0)
    first = me_ref[0] * share_blocks
    for i in range(pieces):

        @pl.when(at // blocks == i)
        def _():
            here = pl.ds(pl.multiple_of((at - i * blocks) * block, block), block)
            basis = jnp.concatenate(
                [factor_refs[s * pieces + i][here, :] for s in range(shards)], axis=1
            )
            slope_ref[...] = jnp.dot(basis, dressed, preferred_element_type=jnp.float32)

            @pl.when((at >= first) & (at < first + share_blocks))
            def _():
                parts = lax.dot_general(
                    trace_ref[...],
                    basis,
                    (((1,), (1,)), ((), ())),
                    preferred_element_type=jnp.float32,
                )
                there = (
                    slice(None)
                    if share_blocks == 1
                    else pl.ds(pl.multiple_of((at - first) * block, block), block)
                )
                collision_ref[:, there] = jnp.sum(parts, axis=0, keepdims=True)


def slope(steps, dressed, traces):
    shards, pieces = len(steps), len(steps[0])
    length, vectors = steps[0][0].shape
    columns = dressed[0].shape[1]
    depth = shards * vectors
    rows = pieces * length
    share = rows // shards
    block = min(length, share, 1024)
    whole = lambda g, me: (0, 0)
    slopes, collision = pl.pallas_call(
        functools.partial(slope_body, shards, pieces, block, share // block),
        grid_spec=pltpu.PrefetchScalarGridSpec(
            num_scalar_prefetch=1,
            grid=(rows // block,),
            in_specs=[IN_VMEM] * (shards * pieces)
            + [pl.BlockSpec((vectors, columns), whole)] * shards
            + [pl.BlockSpec((shards, vectors), whole)] * shards,
            out_specs=[
                pl.BlockSpec((block, columns), lambda g, me: (g, 0)),
                pl.BlockSpec((1, share), whole),
            ],
            scratch_shapes=[pltpu.VMEM((8, depth), jnp.bfloat16)],
        ),
        out_shape=[
            jax.ShapeDtypeStruct((rows, columns), jnp.float32),
            jax.ShapeDtypeStruct((1, share), jnp.float32),
        ],
        compiler_params=pltpu.CompilerParams(vmem_limit_bytes=16 * MIB),
        cost_estimate=pl.CostEstimate(
            flops=2 * rows * depth * columns,
            bytes_accessed=rows * depth * 2 + rows * columns * 4,
            transcendentals=0,
        ),
    )(
        lax.axis_index("aux").astype(jnp.int32)[None],
        *[in_vmem(piece) for step in steps for piece in step],
        *dressed,
        *traces,
    )
    return slopes, collision.reshape(share)


def local(pair_green_block, cholesky_factors, green_one, screening):
    rows, columns = pair_green_block.shape
    vectors = cholesky_factors.shape[1]
    norb = green_one.shape[0]
    orb_count = columns // norb
    aux_size = lax.axis_size("aux")
    me = lax.axis_index("aux")
    length = rows // PIECES

    green, green_one = load(pair_green_block, green_one)
    trace_weights = lax.dynamic_slice_in_dim(
        green_one, me * orb_count, orb_count, 1
    ).T.reshape(1, columns)
    steps, dressed, traced = [], [], []
    for step in range(aux_size):
        total = jnp.zeros((vectors, columns), jnp.float32)
        pieces = []
        for i in range(PIECES):
            first = i * length
            if step == 0:
                piece = lax.slice_in_dim(cholesky_factors, first, first + length, axis=0)
            elif i == 0:
                piece = gate(shifted(steps[-1][i], "aux", 1), dressed[-1], traced[-1])
            else:
                piece = gate(shifted(steps[-1][i], "aux", 1), total)
            pieces.append(piece)
            if step < aux_size - 1:
                total = project(piece, green, first, total)
            else:
                total = total + project_plain(piece, green[first : first + length])
        steps.append(pieces)
        both, trace = sum_and_dress(step, total, screening, green_one, trace_weights)
        dressed.append(both)
        traced.append(trace)

    trace = jnp.concatenate(traced, axis=0)
    traces = [trace] + [shifted(trace, "aux", shift) for shift in range(1, aux_size)]
    return slope(steps, dressed, traces)


def solution(mesh):
    placed = (P("rows", "aux"), P("rows", "aux"), P(), P())
    return jax.shard_map(
        local,
        mesh=mesh,
        in_specs=placed,
        out_specs=(P("rows", "aux"), P(("rows", "aux"))),
        check_vma=False,
    )
```

```python
import functools

import jax
import jax.numpy as jnp
from jax import lax
from jax.experimental import pallas as pl
from jax.experimental.pallas import tpu as pltpu
from jax.sharding import PartitionSpec as P

HIGHEST = lax.Precision.HIGHEST
PIECES = 2
MIB = 1024 * 1024
FREE = pl.CostEstimate(flops=0, bytes_accessed=0, transcendentals=0)
ANYWHERE = pl.BlockSpec(memory_space=pl.ANY)
IN_VMEM = pl.BlockSpec(memory_space=pltpu.VMEM)


vmem_shape = pltpu.VMEM


def in_vmem(block):
    return pltpu.with_memory_space_constraint(block, pltpu.VMEM)


def in_hbm(block):
    return pltpu.with_memory_space_constraint(block, pltpu.HBM)


def shifted(block, axis, shift):
    count = lax.axis_size(axis)
    return lax.ppermute(block, axis, [(i, (i + shift) % count) for i in range(count)])


def exchanged(block, axis, bit):
    count = lax.axis_size(axis)
    return lax.ppermute(block, axis, [(i, i ^ bit) for i in range(count)])


def gate_body(*refs):
    del refs


def gate(block, place, *after):
    return pl.pallas_call(
        gate_body,
        out_shape=jax.ShapeDtypeStruct(block.shape, block.dtype),
        in_specs=[ANYWHERE] * (1 + len(after)),
        out_specs=ANYWHERE,
        input_output_aliases={0: 0},
        compiler_params=pltpu.CompilerParams(vmem_limit_bytes=2 * MIB),
        cost_estimate=FREE,
    )(place(block), *after)


def load_body(count, *refs):
    arrays, copies, semaphores = refs[:count], refs[count : 2 * count], refs[-1]
    moves = [
        pltpu.make_async_copy(array, copy, semaphores.at[i])
        for i, (array, copy) in enumerate(zip(arrays, copies))
    ]
    for move in moves:
        move.start()
    for move in moves:
        move.wait()


def load(*arrays):
    return pl.pallas_call(
        functools.partial(load_body, len(arrays)),
        out_shape=[vmem_shape(array.shape, array.dtype) for array in arrays],
        in_specs=[pl.BlockSpec(memory_space=pltpu.HBM)] * len(arrays),
        out_specs=[IN_VMEM] * len(arrays),
        scratch_shapes=[pltpu.SemaphoreType.DMA((len(arrays),))],
        compiler_params=pltpu.CompilerParams(vmem_limit_bytes=2 * MIB),
        cost_estimate=FREE,
    )(*[in_hbm(array) for array in arrays])


def project_body(first, block, piece_ref, green_ref, acc_ref, total_ref):
    total_ref[...] = acc_ref[...]

    @pl.loop(0, piece_ref.shape[0] // block)
    def _(i):
        at = pl.multiple_of(i * block, block)
        total_ref[...] += lax.dot_general(
            piece_ref[pl.ds(at, block), :],
            green_ref[pl.ds(first + at, block), :],
            (((0,), (0,)), ((), ())),
            preferred_element_type=jnp.float32,
        )


def project(piece, green, first, so_far):
    length, vectors = piece.shape
    columns = green.shape[1]
    return pl.pallas_call(
        functools.partial(project_body, first, min(length, 1024)),
        out_shape=jax.ShapeDtypeStruct((vectors, columns), jnp.float32),
        in_specs=[IN_VMEM] * 3,
        out_specs=IN_VMEM,
        compiler_params=pltpu.CompilerParams(vmem_limit_bytes=6 * MIB),
        cost_estimate=FREE,
    )(piece, green, so_far)


def project_plain(piece, green_rows):
    return lax.dot_general(
        piece, green_rows, (((0,), (0,)), ((), ())), preferred_element_type=jnp.float32
    )


def add_body(left_ref, right_ref, sum_ref):
    sum_ref[...] = left_ref[...] + right_ref[...]


def add(left, right):
    return pl.pallas_call(
        add_body,
        out_shape=jax.ShapeDtypeStruct(left.shape, left.dtype),
        compiler_params=pltpu.CompilerParams(vmem_limit_bytes=4 * MIB),
        cost_estimate=FREE,
    )(in_vmem(left), in_vmem(right))


def dress_body(step, mine_ref, other_ref, weights_ref, green_ref, dressed_ref):
    half = mine_ref.shape[0]
    norb = green_ref.shape[0]
    aux_size = lax.axis_size("aux")
    owner = lax.rem(lax.axis_index("aux") - step + aux_size, aux_size)
    upper = lax.rem(lax.axis_index("rows"), 2)
    weights = weights_ref[pl.ds((owner * 2 + upper) * half, half), :]
    total = mine_ref[...] + other_ref[...]
    green = green_ref[...]
    for first in range(0, total.shape[1], norb):
        mixed = jnp.dot(
            total[:, first : first + norb],
            green,
            precision=HIGHEST,
            preferred_element_type=jnp.float32,
        )
        dressed_ref[:, first : first + norb] = (mixed * weights).astype(jnp.bfloat16)


def dress(step, mine, other, weights, green_one):
    return pl.pallas_call(
        functools.partial(dress_body, step),
        out_shape=jax.ShapeDtypeStruct(mine.shape, jnp.bfloat16),
        compiler_params=pltpu.CompilerParams(vmem_limit_bytes=6 * MIB),
        cost_estimate=FREE,
    )(in_vmem(mine), in_vmem(other), weights, in_vmem(green_one))


def join_body(mine_ref, other_ref, trace_ref, dressed_ref, traced_ref):
    half = mine_ref.shape[0]
    upper = lax.rem(lax.axis_index("rows"), 2)
    dressed_ref[pl.ds(pl.multiple_of(upper * half, half), half), :] = mine_ref[...]
    dressed_ref[pl.ds(pl.multiple_of((1 - upper) * half, half), half), :] = other_ref[...]
    row = trace_ref[...]
    high = row.astype(jnp.bfloat16).astype(jnp.float32)
    middle = (row - high).astype(jnp.bfloat16).astype(jnp.float32)
    parts = jnp.concatenate(
        [row - high - middle, middle, high, jnp.zeros((5, row.shape[1]), jnp.float32)], axis=0
    )
    traced = lax.dot_general(
        parts.astype(jnp.bfloat16),
        dressed_ref[...],
        (((1,), (1,)), ((), ())),
        preferred_element_type=jnp.float32,
    )
    traced_ref[...] = jnp.sum(traced, axis=0, keepdims=True)


def join(mine, other, trace_weights):
    half, columns = mine.shape
    return pl.pallas_call(
        join_body,
        out_shape=[
            jax.ShapeDtypeStruct((2 * half, columns), jnp.bfloat16),
            jax.ShapeDtypeStruct((1, 2 * half), jnp.float32),
        ],
        compiler_params=pltpu.CompilerParams(vmem_limit_bytes=6 * MIB),
        cost_estimate=FREE,
    )(in_vmem(mine), in_vmem(other), trace_weights)


def sum_and_dress(step, projection, weights, green_one, trace_weights):
    count = lax.axis_size("rows")
    half = projection.shape[0] // 2
    upper = lax.rem(lax.axis_index("rows"), 2) == 1
    low, high = projection[:half], projection[half:]
    total = jnp.where(upper, high, low)
    other = exchanged(jnp.where(upper, low, high), "rows", 1)
    bit = 2
    while bit < count:
        total = add(total, other)
        other = exchanged(total, "rows", bit)
        bit *= 2
    mine = dress(step, total, other, weights, green_one)
    return join(mine, exchanged(mine, "rows", 1), trace_weights)


SLOTS = 3
PARTS = 4


def slope_body(shards, pieces, steps, share_blocks, me_ref, *refs):
    count = 1 + (shards - 1) * pieces
    factor_refs = refs[:count]
    dressed_refs = refs[count : count + shards]
    trace_refs = refs[count + shards : count + 2 * shards]
    slope_ref, collision_ref, trace_ref, dressed_ref, held_ref, semaphores = refs[count + 2 * shards :]
    at = pl.program_id(0)
    block = held_ref.shape[1]
    part = block // PARTS

    def copies(step):
        slot = lax.rem(step, SLOTS)
        return [
            pltpu.make_async_copy(
                held_ref.at[slot, pl.ds(i * part, part), :],
                slope_ref.at[pl.ds(pl.multiple_of(step * block, block) + i * part, part), :],
                semaphores.at[slot, i],
            )
            for i in range(PARTS)
        ]

    @pl.when(at == 0)
    def _():
        trace = trace_refs[0][...]
        for shift in range(1, shards):
            came = trace_refs[shift][...]
            trace = trace + jnp.concatenate(
                [came[shards - shift :], came[: shards - shift]], axis=0
            )
        row = jnp.concatenate([trace[s : s + 1] for s in range(shards)], axis=1)
        high = row.astype(jnp.bfloat16).astype(jnp.float32)
        middle = (row - high).astype(jnp.bfloat16).astype(jnp.float32)
        low = row - high - middle
        trace_ref[...] = jnp.concatenate(
            [low, middle, high, jnp.zeros((5, row.shape[1]), jnp.float32)], axis=0
        ).astype(jnp.bfloat16)
        dressed_ref[...] = jnp.concatenate([ref[...] for ref in dressed_refs], axis=0)

    @pl.when(at >= SLOTS)
    def _():
        for copy in copies(at - SLOTS):
            copy.wait()

    first = me_ref[0] * share_blocks
    slot = lax.rem(at, SLOTS)
    for i in range(pieces):

        @pl.when(at // (steps // pieces) == i)
        def _():
            basis = jnp.concatenate(
                [factor_refs[0][...]]
                + [factor_refs[1 + s * pieces + i][...] for s in range(shards - 1)],
                axis=1,
            )
            held_ref[slot] = jnp.dot(
                basis, dressed_ref[...], preferred_element_type=jnp.float32
            )

            @pl.when((at >= first) & (at < first + share_blocks))
            def _():
                parts = lax.dot_general(
                    trace_ref[...],
                    basis,
                    (((1,), (1,)), ((), ())),
                    preferred_element_type=jnp.float32,
                )
                there = (
                    slice(None)
                    if share_blocks == 1
                    else pl.ds(pl.multiple_of((at - first) * block, block), block)
                )
                collision_ref[:, there] = jnp.sum(parts, axis=0, keepdims=True)

    for copy in copies(at):
        copy.start()

    @pl.when(at == steps - 1)
    def _():
        for back in range(min(SLOTS, steps) - 1, -1, -1):
            for copy in copies(at - back):
                copy.wait()


def slope(own, steps, dressed, traces):
    shards, pieces = len(dressed), len(steps[0])
    rows, vectors = own.shape
    columns = dressed[0].shape[1]
    depth = shards * vectors
    share = rows // shards
    block = min(rows // pieces, share, 1024)
    blocks = rows // pieces // block
    whole = lambda g, me: (0, 0)
    factor_specs = [pl.BlockSpec((block, vectors), lambda g, me: (g, 0))] + [
        pl.BlockSpec(
            (block, vectors), lambda g, me, i=i: (jnp.clip(g - i * blocks, 0, blocks - 1), 0)
        )
        for _ in steps
        for i in range(pieces)
    ]
    slopes, collision = pl.pallas_call(
        functools.partial(slope_body, shards, pieces, rows // block, share // block),
        grid_spec=pltpu.PrefetchScalarGridSpec(
            num_scalar_prefetch=1,
            grid=(rows // block,),
            in_specs=factor_specs
            + [pl.BlockSpec((vectors, columns), whole)] * shards
            + [pl.BlockSpec((shards, vectors), whole)] * shards,
            out_specs=[
                pl.BlockSpec(memory_space=pl.ANY),
                pl.BlockSpec((1, share), whole),
            ],
            scratch_shapes=[
                pltpu.VMEM((8, depth), jnp.bfloat16),
                pltpu.VMEM((depth, columns), jnp.bfloat16),
                pltpu.VMEM((SLOTS, block, columns), jnp.float32),
                pltpu.SemaphoreType.DMA((SLOTS, PARTS)),
            ],
        ),
        out_shape=[
            jax.ShapeDtypeStruct((rows, columns), jnp.float32),
            jax.ShapeDtypeStruct((1, share), jnp.float32),
        ],
        compiler_params=pltpu.CompilerParams(vmem_limit_bytes=24 * MIB),
        cost_estimate=pl.CostEstimate(
            flops=2 * rows * depth * columns,
            bytes_accessed=rows * depth * 2 + rows * columns * 4,
            transcendentals=0,
        ),
    )(
        lax.axis_index("aux").astype(jnp.int32)[None],
        in_hbm(own),
        *[in_hbm(piece) for step in steps[:-1] for piece in step],
        *[in_vmem(piece) for piece in steps[-1]],
        *[in_hbm(both) for both in dressed[:-1]],
        in_vmem(dressed[-1]),
        *traces,
    )
    return slopes, collision.reshape(share)


def local(pair_green_block, cholesky_factors, green_one, screening):
    rows, columns = pair_green_block.shape
    vectors = cholesky_factors.shape[1]
    norb = green_one.shape[0]
    orb_count = columns // norb
    aux_size = lax.axis_size("aux")
    me = lax.axis_index("aux")
    length = rows // PIECES

    green, green_one = load(pair_green_block, green_one)
    trace_weights = lax.dynamic_slice_in_dim(
        green_one, me * orb_count, orb_count, 1
    ).T.reshape(1, columns)
    weights = screening[:, None]
    zeros = jnp.zeros((vectors, columns), jnp.float32)

    dressed, traced = [], []

    def finish(step, total):
        both, trace = sum_and_dress(step, total, weights, green_one, trace_weights)
        dressed.append(both)
        traced.append(trace)

    held = [
        lax.slice_in_dim(cholesky_factors, i * length, (i + 1) * length, axis=0)
        for i in range(PIECES)
    ]
    finish(0, project(cholesky_factors, green, 0, zeros))
    steps = []
    for step in range(1, aux_size):
        total, pieces = zeros, []
        for i in range(PIECES):
            after = (dressed[-1], traced[-1]) if i == 0 else (total,)
            place = in_hbm if step < aux_size - 1 else in_vmem
            piece = gate(shifted(held[i], "aux", 1), place, *after)
            pieces.append(piece)
            first = i * length
            if step < aux_size - 1:
                total = project(piece, green, first, total)
            else:
                total = total + project_plain(piece, green[first : first + length])
        held = pieces
        steps.append(pieces)
        finish(step, total)

    trace = jnp.concatenate(traced, axis=0)
    traces = [trace] + [shifted(trace, "aux", shift) for shift in range(1, aux_size)]
    return slope(cholesky_factors, steps, dressed, traces)


def solution(mesh):
    placed = (P("rows", "aux"), P("rows", "aux"), P(), P())
    return jax.shard_map(
        local,
        mesh=mesh,
        in_specs=placed,
        out_specs=(P("rows", "aux"), P(("rows", "aux"))),
        check_vma=False,
    )
```

```python
import functools

import jax
import jax.numpy as jnp
from jax import lax
from jax.experimental import pallas as pl
from jax.experimental.pallas import tpu as pltpu
from jax.sharding import PartitionSpec as P

HIGHEST = lax.Precision.HIGHEST
PIECES = 2
MIB = 1024 * 1024
FREE = pl.CostEstimate(flops=0, bytes_accessed=0, transcendentals=0)
ANYWHERE = pl.BlockSpec(memory_space=pl.ANY)
IN_VMEM = pl.BlockSpec(memory_space=pltpu.VMEM)


vmem_shape = pltpu.VMEM


def in_vmem(block):
    return pltpu.with_memory_space_constraint(block, pltpu.VMEM)


def in_hbm(block):
    return pltpu.with_memory_space_constraint(block, pltpu.HBM)


def shifted(block, axis, shift):
    count = lax.axis_size(axis)
    return lax.ppermute(block, axis, [(i, (i + shift) % count) for i in range(count)])


def exchanged(block, axis, bit):
    count = lax.axis_size(axis)
    return lax.ppermute(block, axis, [(i, i ^ bit) for i in range(count)])


def gate_body(*refs):
    del refs


def gate(block, place, *after):
    return pl.pallas_call(
        gate_body,
        out_shape=jax.ShapeDtypeStruct(block.shape, block.dtype),
        in_specs=[ANYWHERE] * (1 + len(after)),
        out_specs=ANYWHERE,
        input_output_aliases={0: 0},
        compiler_params=pltpu.CompilerParams(vmem_limit_bytes=2 * MIB),
        cost_estimate=FREE,
    )(place(block), *after)


def load_body(count, *refs):
    arrays, copies, semaphores = refs[:count], refs[count : 2 * count], refs[-1]
    moves = [
        pltpu.make_async_copy(array, copy, semaphores.at[i])
        for i, (array, copy) in enumerate(zip(arrays, copies))
    ]
    for move in moves:
        move.start()
    for move in moves:
        move.wait()


def load(*arrays):
    return pl.pallas_call(
        functools.partial(load_body, len(arrays)),
        out_shape=[vmem_shape(array.shape, array.dtype) for array in arrays],
        in_specs=[pl.BlockSpec(memory_space=pltpu.HBM)] * len(arrays),
        out_specs=[IN_VMEM] * len(arrays),
        scratch_shapes=[pltpu.SemaphoreType.DMA((len(arrays),))],
        compiler_params=pltpu.CompilerParams(vmem_limit_bytes=2 * MIB),
        cost_estimate=FREE,
    )(*[in_hbm(array) for array in arrays])


def cut_body(first, array_ref, piece_ref, semaphore):
    move = pltpu.make_async_copy(
        array_ref.at[pl.ds(first, piece_ref.shape[0]), :], piece_ref, semaphore
    )
    move.start()
    move.wait()


def cut(array, first, length):
    return pl.pallas_call(
        functools.partial(cut_body, first),
        out_shape=vmem_shape((length,) + array.shape[1:], array.dtype),
        in_specs=[pl.BlockSpec(memory_space=pltpu.HBM)],
        out_specs=IN_VMEM,
        scratch_shapes=[pltpu.SemaphoreType.DMA],
        compiler_params=pltpu.CompilerParams(vmem_limit_bytes=2 * MIB),
        cost_estimate=FREE,
    )(in_hbm(array))


def project_body(first, block, piece_ref, green_ref, acc_ref, total_ref):
    total_ref[...] = acc_ref[...]

    @pl.loop(0, piece_ref.shape[0] // block)
    def _(i):
        at = pl.multiple_of(i * block, block)
        total_ref[...] += lax.dot_general(
            piece_ref[pl.ds(at, block), :],
            green_ref[pl.ds(first + at, block), :],
            (((0,), (0,)), ((), ())),
            preferred_element_type=jnp.float32,
        )


def project(piece, green, first, so_far):
    length, vectors = piece.shape
    columns = green.shape[1]
    return pl.pallas_call(
        functools.partial(project_body, first, min(length, 1024)),
        out_shape=jax.ShapeDtypeStruct((vectors, columns), jnp.float32),
        in_specs=[IN_VMEM] * 3,
        out_specs=IN_VMEM,
        compiler_params=pltpu.CompilerParams(vmem_limit_bytes=6 * MIB),
        cost_estimate=FREE,
    )(piece, green, so_far)


def project_plain(piece, green_rows):
    return lax.dot_general(
        piece, green_rows, (((0,), (0,)), ((), ())), preferred_element_type=jnp.float32
    )


def add_up(arrays):
    while len(arrays) > 1:
        arrays = [arrays[i] + arrays[i + 1] for i in range(0, len(arrays), 2)]
    return arrays[0]


def add_body(*refs):
    refs[-1][...] = add_up([ref[...] for ref in refs[:-1]])


def add(*arrays):
    return pl.pallas_call(
        add_body,
        out_shape=jax.ShapeDtypeStruct(arrays[0].shape, arrays[0].dtype),
        compiler_params=pltpu.CompilerParams(vmem_limit_bytes=4 * MIB),
        cost_estimate=FREE,
    )(*[in_vmem(array) for array in arrays])


def dress_body(step, *refs):
    summand_refs, (weights_ref, green_ref, dressed_ref) = refs[:-3], refs[-3:]
    half = dressed_ref.shape[0]
    norb = green_ref.shape[0]
    aux_size = lax.axis_size("aux")
    owner = lax.rem(lax.axis_index("aux") - step + aux_size, aux_size)
    upper = lax.rem(lax.axis_index("rows"), 2)
    weights = weights_ref[pl.ds((owner * 2 + upper) * half, half), :]
    total = add_up([ref[...] for ref in summand_refs])
    green = green_ref[...]
    for first in range(0, total.shape[1], norb):
        mixed = jnp.dot(
            total[:, first : first + norb],
            green,
            precision=HIGHEST,
            preferred_element_type=jnp.float32,
        )
        dressed_ref[:, first : first + norb] = (mixed * weights).astype(jnp.bfloat16)


def dress(step, summands, weights, green_one):
    return pl.pallas_call(
        functools.partial(dress_body, step),
        out_shape=jax.ShapeDtypeStruct(summands[0].shape, jnp.bfloat16),
        compiler_params=pltpu.CompilerParams(vmem_limit_bytes=6 * MIB),
        cost_estimate=FREE,
    )(*[in_vmem(summand) for summand in summands], weights, in_vmem(green_one))


def join_body(mine_ref, other_ref, trace_ref, dressed_ref, traced_ref):
    half = mine_ref.shape[0]
    upper = lax.rem(lax.axis_index("rows"), 2)
    dressed_ref[pl.ds(pl.multiple_of(upper * half, half), half), :] = mine_ref[...]
    dressed_ref[pl.ds(pl.multiple_of((1 - upper) * half, half), half), :] = other_ref[...]
    row = trace_ref[...]
    high = row.astype(jnp.bfloat16).astype(jnp.float32)
    middle = (row - high).astype(jnp.bfloat16).astype(jnp.float32)
    parts = jnp.concatenate(
        [row - high - middle, middle, high, jnp.zeros((5, row.shape[1]), jnp.float32)], axis=0
    )
    traced = lax.dot_general(
        parts.astype(jnp.bfloat16),
        dressed_ref[...],
        (((1,), (1,)), ((), ())),
        preferred_element_type=jnp.float32,
    )
    traced_ref[...] = jnp.sum(traced, axis=0, keepdims=True)


def join(mine, other, trace_weights):
    half, columns = mine.shape
    return pl.pallas_call(
        join_body,
        out_shape=[
            jax.ShapeDtypeStruct((2 * half, columns), jnp.bfloat16),
            jax.ShapeDtypeStruct((1, 2 * half), jnp.float32),
        ],
        compiler_params=pltpu.CompilerParams(vmem_limit_bytes=6 * MIB),
        cost_estimate=FREE,
    )(in_vmem(mine), in_vmem(other), trace_weights)


def sum_and_dress(step, projection, weights, green_one, trace_weights):
    count = lax.axis_size("rows")
    half = projection.shape[0] // 2
    upper = lax.rem(lax.axis_index("rows"), 2) == 1
    low, high = projection[:half], projection[half:]
    summands = [
        jnp.where(upper, high, low),
        exchanged(jnp.where(upper, low, high), "rows", 1),
    ]
    bits = [1 << b for b in range(1, count.bit_length() - 1)]
    while bits:
        total = add(*summands)
        partners = [bits[0]] if len(bits) == 1 else [bits[0], bits[1], bits[0] ^ bits[1]]
        summands = [total] + [exchanged(total, "rows", partner) for partner in partners]
        bits = bits[2:]
    mine = dress(step, summands, weights, green_one)
    return join(mine, exchanged(mine, "rows", 1), trace_weights)


SLOTS = 3
PARTS = 2


def slope_body(pieces, me_ref, *refs):
    slope_ref, collision_ref, factors_ref, dressed_ref, held_ref, came, gone = refs[-7:]
    shards = factors_ref.shape[0] + 1
    early = 1 + (shards - 2) * pieces
    early_refs, last_refs = refs[:early], refs[early : early + pieces]
    dressed_refs = refs[early + pieces : early + pieces + shards]
    trace_refs = refs[early + pieces + shards : early + pieces + 2 * shards]
    rows = factors_ref.shape[1]
    block = held_ref.shape[1]
    steps, length = rows // block, rows // pieces
    share_blocks = rows // shards // block
    part = block // PARTS

    def arrivals(at):
        first = at * block
        sources = [early_refs[0].at[pl.ds(first, block), :]] + [
            early_refs[1 + s * pieces + first // length].at[pl.ds(first % length, block), :]
            for s in range(shards - 2)
        ]
        return [
            pltpu.make_async_copy(
                source, factors_ref.at[s, pl.ds(first, block), :], came.at[at, s]
            )
            for s, source in enumerate(sources)
        ]

    def departures(at):
        return [
            pltpu.make_async_copy(
                held_ref.at[at % SLOTS, pl.ds(i * part, part), :],
                slope_ref.at[pl.ds(at * block + i * part, part), :],
                gone.at[at % SLOTS, i],
            )
            for i in range(PARTS)
        ]

    for at in range(steps):
        for copy in arrivals(at):
            copy.start()

    trace = trace_refs[0][...]
    for shift in range(1, shards):
        other = trace_refs[shift][...]
        trace = trace + jnp.concatenate([other[shards - shift :], other[: shards - shift]], axis=0)
    row = jnp.concatenate([trace[s : s + 1] for s in range(shards)], axis=1)
    high = row.astype(jnp.bfloat16).astype(jnp.float32)
    middle = (row - high).astype(jnp.bfloat16).astype(jnp.float32)
    low = row - high - middle
    thirds = jnp.concatenate(
        [low, middle, high, jnp.zeros((5, row.shape[1]), jnp.float32)], axis=0
    ).astype(jnp.bfloat16)
    dressed_ref[...] = jnp.concatenate([ref[...] for ref in dressed_refs], axis=0)

    for at in range(steps):
        for copy in arrivals(at):
            copy.wait()
        if at >= SLOTS:
            for copy in departures(at - SLOTS):
                copy.wait()
        first = at * block
        basis = jnp.concatenate(
            [factors_ref[s, pl.ds(first, block), :] for s in range(shards - 1)]
            + [last_refs[first // length][pl.ds(first % length, block), :]],
            axis=1,
        )
        held_ref[at % SLOTS] = jnp.dot(
            basis, dressed_ref[...], preferred_element_type=jnp.float32
        )
        for copy in departures(at):
            copy.start()

        @pl.when(me_ref[0] == at // share_blocks)
        def _():
            parts = lax.dot_general(
                thirds, basis, (((1,), (1,)), ((), ())), preferred_element_type=jnp.float32
            )
            there = pl.ds(at % share_blocks * block, block)
            collision_ref[:, there] = jnp.sum(parts, axis=0, keepdims=True)

    for at in range(max(steps - SLOTS, 0), steps):
        for copy in departures(at):
            copy.wait()


def slope(own, steps, dressed, traces):
    shards, pieces = len(dressed), len(steps[0])
    rows, vectors = own.shape
    columns = dressed[0].shape[1]
    depth = shards * vectors
    share = rows // shards
    block = min(rows // pieces, share, 1024)
    far = pl.BlockSpec(memory_space=pltpu.HBM)
    early = [own] + [piece for step in steps[:-1] for piece in step]
    near = [*steps[-1], *dressed, *traces]
    slopes, collision = pl.pallas_call(
        functools.partial(slope_body, pieces),
        in_specs=[pl.BlockSpec(memory_space=pltpu.SMEM)]
        + [far] * len(early)
        + [IN_VMEM] * len(near),
        out_specs=[far, IN_VMEM],
        scratch_shapes=[
            pltpu.VMEM((shards - 1, rows, vectors), jnp.bfloat16),
            pltpu.VMEM((depth, columns), jnp.bfloat16),
            pltpu.VMEM((SLOTS, block, columns), jnp.float32),
            pltpu.SemaphoreType.DMA((rows // block, shards - 1)),
            pltpu.SemaphoreType.DMA((SLOTS, PARTS)),
        ],
        out_shape=[
            jax.ShapeDtypeStruct((rows, columns), jnp.float32),
            jax.ShapeDtypeStruct((1, share), jnp.float32),
        ],
        compiler_params=pltpu.CompilerParams(vmem_limit_bytes=28 * MIB),
        cost_estimate=pl.CostEstimate(
            flops=2 * rows * depth * columns,
            bytes_accessed=rows * depth * 2 + rows * columns * 4,
            transcendentals=0,
        ),
    )(
        lax.axis_index("aux").astype(jnp.int32)[None],
        *[in_hbm(piece) for piece in early],
        *[in_vmem(piece) for piece in steps[-1]],
        *[in_vmem(both) for both in dressed],
        *traces,
    )
    return slopes, collision.reshape(share)


def local(pair_green_block, cholesky_factors, green_one, screening):
    rows, columns = pair_green_block.shape
    vectors = cholesky_factors.shape[1]
    norb = green_one.shape[0]
    orb_count = columns // norb
    aux_size = lax.axis_size("aux")
    me = lax.axis_index("aux")
    length = rows // PIECES

    green, green_one = load(pair_green_block, green_one)
    trace_weights = lax.dynamic_slice_in_dim(
        green_one, me * orb_count, orb_count, 1
    ).T.reshape(1, columns)
    weights = screening[:, None]
    zeros = jnp.zeros((vectors, columns), jnp.float32)

    dressed, traced = [], []

    def finish(step, total):
        both, trace = sum_and_dress(step, total, weights, green_one, trace_weights)
        dressed.append(both)
        traced.append(trace)

    held = [cut(cholesky_factors, i * length, length) for i in range(PIECES)]
    finish(0, project(cholesky_factors, green, 0, zeros))
    steps = []
    for step in range(1, aux_size):
        total, pieces = zeros, []
        for i in range(PIECES):
            after = (dressed[-1], traced[-1]) if i == 0 else (total,)
            place = in_hbm if step < aux_size - 1 else in_vmem
            piece = gate(shifted(held[i], "aux", 1), place, *after)
            pieces.append(piece)
            first = i * length
            if step < aux_size - 1:
                total = project(piece, green, first, total)
            else:
                total = total + project_plain(piece, green[first : first + length])
        held = pieces
        steps.append(pieces)
        finish(step, total)

    trace = jnp.concatenate(traced, axis=0)
    traces = [trace] + [shifted(trace, "aux", shift) for shift in range(1, aux_size)]
    return slope(cholesky_factors, steps, dressed, traces)


def solution(mesh):
    placed = (P("rows", "aux"), P("rows", "aux"), P(), P())
    return jax.shard_map(
        local,
        mesh=mesh,
        in_specs=placed,
        out_specs=(P("rows", "aux"), P(("rows", "aux"))),
        check_vma=False,
    )
```

```python
import functools

import jax
import jax.numpy as jnp
from jax import lax
from jax.experimental import pallas as pl
from jax.experimental.pallas import tpu as pltpu
from jax.sharding import PartitionSpec as P

HIGHEST = lax.Precision.HIGHEST
PIECES = 2
MIB = 1024 * 1024
FREE = pl.CostEstimate(flops=0, bytes_accessed=0, transcendentals=0)
ANYWHERE = pl.BlockSpec(memory_space=pl.ANY)
IN_VMEM = pl.BlockSpec(memory_space=pltpu.VMEM)


vmem_shape = pltpu.VMEM


def in_vmem(block):
    return pltpu.with_memory_space_constraint(block, pltpu.VMEM)


def in_hbm(block):
    return pltpu.with_memory_space_constraint(block, pltpu.HBM)


def shifted(block, axis, shift):
    count = lax.axis_size(axis)
    return lax.ppermute(block, axis, [(i, (i + shift) % count) for i in range(count)])


def exchanged(block, axis, bit):
    count = lax.axis_size(axis)
    return lax.ppermute(block, axis, [(i, i ^ bit) for i in range(count)])


def gate_body(*refs):
    del refs


def gate(block, place, *after):
    return pl.pallas_call(
        gate_body,
        out_shape=jax.ShapeDtypeStruct(block.shape, block.dtype),
        in_specs=[ANYWHERE] * (1 + len(after)),
        out_specs=ANYWHERE,
        input_output_aliases={0: 0},
        compiler_params=pltpu.CompilerParams(vmem_limit_bytes=2 * MIB),
        cost_estimate=FREE,
    )(place(block), *after)


def load_body(count, *refs):
    arrays, copies, semaphores = refs[:count], refs[count : 2 * count], refs[-1]
    moves = [
        pltpu.make_async_copy(array, copy, semaphores.at[i])
        for i, (array, copy) in enumerate(zip(arrays, copies))
    ]
    for move in moves:
        move.start()
    for move in moves:
        move.wait()


def load(*arrays):
    return pl.pallas_call(
        functools.partial(load_body, len(arrays)),
        out_shape=[vmem_shape(array.shape, array.dtype) for array in arrays],
        in_specs=[pl.BlockSpec(memory_space=pltpu.HBM)] * len(arrays),
        out_specs=[IN_VMEM] * len(arrays),
        scratch_shapes=[pltpu.SemaphoreType.DMA((len(arrays),))],
        compiler_params=pltpu.CompilerParams(vmem_limit_bytes=2 * MIB),
        cost_estimate=FREE,
    )(*[in_hbm(array) for array in arrays])


def cut_body(first, array_ref, piece_ref, semaphores):
    parts = semaphores.shape[0]
    part = piece_ref.shape[0] // parts
    moves = [
        pltpu.make_async_copy(
            array_ref.at[pl.ds(first + i * part, part), :],
            piece_ref.at[pl.ds(i * part, part), :],
            semaphores.at[i],
        )
        for i in range(parts)
    ]
    for move in moves:
        move.start()
    for move in moves:
        move.wait()


def cut(array, first, length):
    return pl.pallas_call(
        functools.partial(cut_body, first),
        out_shape=vmem_shape((length,) + array.shape[1:], array.dtype),
        in_specs=[pl.BlockSpec(memory_space=pltpu.HBM)],
        out_specs=IN_VMEM,
        scratch_shapes=[pltpu.SemaphoreType.DMA((4,))],
        compiler_params=pltpu.CompilerParams(vmem_limit_bytes=2 * MIB),
        cost_estimate=FREE,
    )(in_hbm(array))


def project_body(first, block, piece_ref, green_ref, acc_ref, total_ref):
    total_ref[...] = acc_ref[...]

    @pl.loop(0, piece_ref.shape[0] // block)
    def _(i):
        at = pl.multiple_of(i * block, block)
        total_ref[...] += lax.dot_general(
            piece_ref[pl.ds(at, block), :],
            green_ref[pl.ds(first + at, block), :],
            (((0,), (0,)), ((), ())),
            preferred_element_type=jnp.float32,
        )


def project(piece, green, first, so_far):
    length, vectors = piece.shape
    columns = green.shape[1]
    return pl.pallas_call(
        functools.partial(project_body, first, min(length, 1024)),
        out_shape=jax.ShapeDtypeStruct((vectors, columns), jnp.float32),
        in_specs=[IN_VMEM] * 3,
        out_specs=IN_VMEM,
        compiler_params=pltpu.CompilerParams(vmem_limit_bytes=6 * MIB),
        cost_estimate=FREE,
    )(piece, green, so_far)


def project_plain(piece, green_rows):
    return lax.dot_general(
        piece, green_rows, (((0,), (0,)), ((), ())), preferred_element_type=jnp.float32
    )


def add_body(parts, *refs):
    pairs = refs[:-parts]
    sums = [pairs[i][...] + pairs[i + 1][...] for i in range(0, len(pairs), 2)]
    total = sums[0] if len(sums) == 1 else jnp.concatenate(sums, axis=0)
    length = total.shape[0] // parts
    for i in range(parts):
        refs[i - parts][...] = total[i * length : (i + 1) * length]


def add(*pairs):
    rows = sum(array.shape[0] for array in pairs) // 4
    shape = jax.ShapeDtypeStruct((rows,) + pairs[0].shape[1:], pairs[0].dtype)
    return pl.pallas_call(
        functools.partial(add_body, 2),
        out_shape=[shape] * 2,
        compiler_params=pltpu.CompilerParams(vmem_limit_bytes=4 * MIB),
        cost_estimate=FREE,
    )(*[in_vmem(array) for array in pairs])


def dress_body(step, *refs):
    summand_refs, (weights_ref, green_ref, dressed_ref) = refs[:-3], refs[-3:]
    half = dressed_ref.shape[0]
    norb = green_ref.shape[0]
    aux_size = lax.axis_size("aux")
    owner = lax.rem(lax.axis_index("aux") - step + aux_size, aux_size)
    upper = lax.rem(lax.axis_index("rows"), 2)
    weights = weights_ref[pl.ds((owner * 2 + upper) * half, half), :]
    total = jnp.concatenate(
        [
            summand_refs[i][...] + summand_refs[i + 1][...]
            for i in range(0, len(summand_refs), 2)
        ],
        axis=0,
    )
    green = green_ref[...]
    for first in range(0, total.shape[1], norb):
        mixed = jnp.dot(
            total[:, first : first + norb],
            green,
            precision=HIGHEST,
            preferred_element_type=jnp.float32,
        )
        dressed_ref[:, first : first + norb] = (mixed * weights).astype(jnp.bfloat16)


def dress(step, pairs, weights, green_one):
    rows = sum(array.shape[0] for array in pairs) // 2
    return pl.pallas_call(
        functools.partial(dress_body, step),
        out_shape=jax.ShapeDtypeStruct((rows, pairs[0].shape[1]), jnp.bfloat16),
        compiler_params=pltpu.CompilerParams(vmem_limit_bytes=6 * MIB),
        cost_estimate=FREE,
    )(*[in_vmem(array) for array in pairs], weights, in_vmem(green_one))


def join_body(mine_ref, other_ref, trace_ref, dressed_ref, traced_ref):
    half = mine_ref.shape[0]
    upper = lax.rem(lax.axis_index("rows"), 2)
    dressed_ref[pl.ds(pl.multiple_of(upper * half, half), half), :] = mine_ref[...]
    dressed_ref[pl.ds(pl.multiple_of((1 - upper) * half, half), half), :] = other_ref[...]
    row = trace_ref[...]
    high = row.astype(jnp.bfloat16).astype(jnp.float32)
    middle = (row - high).astype(jnp.bfloat16).astype(jnp.float32)
    parts = jnp.concatenate(
        [row - high - middle, middle, high, jnp.zeros((5, row.shape[1]), jnp.float32)], axis=0
    )
    traced = lax.dot_general(
        parts.astype(jnp.bfloat16),
        dressed_ref[...],
        (((1,), (1,)), ((), ())),
        preferred_element_type=jnp.float32,
    )
    traced_ref[...] = jnp.sum(traced, axis=0, keepdims=True)


def join(mine, other, trace_weights):
    half, columns = mine.shape
    return pl.pallas_call(
        join_body,
        out_shape=[
            jax.ShapeDtypeStruct((2 * half, columns), jnp.bfloat16),
            jax.ShapeDtypeStruct((1, 2 * half), jnp.float32),
        ],
        compiler_params=pltpu.CompilerParams(vmem_limit_bytes=6 * MIB),
        cost_estimate=FREE,
    )(in_vmem(mine), in_vmem(other), trace_weights)


def sum_and_dress(step, projection, weights, green_one, trace_weights):
    count = lax.axis_size("rows")
    half = projection.shape[0] // 2
    upper = lax.rem(lax.axis_index("rows"), 2) == 1
    low, high = projection[:half], projection[half:]
    pairs = [
        jnp.where(upper, high, low),
        exchanged(jnp.where(upper, low, high), "rows", 1),
    ]
    bits = [1 << b for b in range(1, count.bit_length() - 1)]
    for i, bit in enumerate(bits):
        other_bit = bits[i ^ 1] if i ^ 1 < len(bits) else bit
        first, second = add(*pairs)
        pairs = [
            first,
            exchanged(first, "rows", bit),
            second,
            exchanged(second, "rows", other_bit),
        ]
    mine = dress(step, pairs, weights, green_one)
    return join(mine, exchanged(mine, "rows", 1), trace_weights)


SLOTS = 4


def slope_body(pieces, me_ref, *refs):
    slope_ref, collision_ref, factors_ref, dressed_ref, held_ref, came, gone = refs[-7:]
    shards = factors_ref.shape[0] + 1
    early = 1 + (shards - 2) * pieces
    early_refs, last_refs = refs[:early], refs[early : early + pieces]
    dressed_refs = refs[early + pieces : early + pieces + shards]
    trace_refs = refs[early + pieces + shards : early + pieces + 2 * shards]
    rows = factors_ref.shape[1]
    chunk, block = rows // came.shape[0], held_ref.shape[1]
    steps, length = rows // block, rows // pieces
    share_blocks = rows // shards // block

    def arrivals(at):
        first = at * chunk
        sources = [early_refs[0].at[pl.ds(first, chunk), :]] + [
            early_refs[1 + s * pieces + first // length].at[pl.ds(first % length, chunk), :]
            for s in range(shards - 2)
        ]
        return [
            pltpu.make_async_copy(
                source, factors_ref.at[s, pl.ds(first, chunk), :], came.at[at, s]
            )
            for s, source in enumerate(sources)
        ]

    def departure(at):
        return pltpu.make_async_copy(
            held_ref.at[at % SLOTS], slope_ref.at[pl.ds(at * block, block), :], gone.at[at % SLOTS]
        )

    for at in range(rows // chunk):
        for copy in arrivals(at):
            copy.start()

    me = me_ref[0]
    rows_of_trace = []
    for s in range(shards):
        total = trace_refs[0][s : s + 1, :]
        for bits in range(1, shards):
            theirs = lax.rem((me ^ bits) - me + s + shards, shards)
            total = total + trace_refs[bits][pl.ds(theirs, 1), :]
        rows_of_trace.append(total)
    row = jnp.concatenate(rows_of_trace, axis=1)
    high = row.astype(jnp.bfloat16).astype(jnp.float32)
    middle = (row - high).astype(jnp.bfloat16).astype(jnp.float32)
    low = row - high - middle
    thirds = jnp.concatenate(
        [low, middle, high, jnp.zeros((5, row.shape[1]), jnp.float32)], axis=0
    ).astype(jnp.bfloat16)
    dressed_ref[...] = jnp.concatenate([ref[...] for ref in dressed_refs], axis=0)

    for at in range(steps):
        if at * block % chunk == 0:
            for copy in arrivals(at * block // chunk):
                copy.wait()
        if at >= SLOTS:
            departure(at - SLOTS).wait()
        first = at * block
        basis = jnp.concatenate(
            [factors_ref[s, pl.ds(first, block), :] for s in range(shards - 1)]
            + [last_refs[first // length][pl.ds(first % length, block), :]],
            axis=1,
        )
        held_ref[at % SLOTS] = jnp.dot(
            basis, dressed_ref[...], preferred_element_type=jnp.float32
        )
        departure(at).start()

        @pl.when(me == at // share_blocks)
        def _():
            parts = lax.dot_general(
                thirds, basis, (((1,), (1,)), ((), ())), preferred_element_type=jnp.float32
            )
            there = pl.ds(at % share_blocks * block, block)
            collision_ref[:, there] = jnp.sum(parts, axis=0, keepdims=True)

    for at in range(max(steps - SLOTS, 0), steps):
        departure(at).wait()


def slope(own, steps, dressed, traces):
    shards, pieces = len(dressed), len(steps[0])
    rows, vectors = own.shape
    columns = dressed[0].shape[1]
    depth = shards * vectors
    share = rows // shards
    chunk = min(rows // pieces, share, 1024)
    block = min(chunk, 512)
    far = pl.BlockSpec(memory_space=pltpu.HBM)
    early = [own] + [piece for step in steps[:-1] for piece in step]
    near = [*steps[-1], *dressed, *traces]
    slopes, collision = pl.pallas_call(
        functools.partial(slope_body, pieces),
        in_specs=[pl.BlockSpec(memory_space=pltpu.SMEM)]
        + [far] * len(early)
        + [IN_VMEM] * len(near),
        out_specs=[far, IN_VMEM],
        scratch_shapes=[
            pltpu.VMEM((shards - 1, rows, vectors), jnp.bfloat16),
            pltpu.VMEM((depth, columns), jnp.bfloat16),
            pltpu.VMEM((SLOTS, block, columns), jnp.float32),
            pltpu.SemaphoreType.DMA((rows // chunk, shards - 1)),
            pltpu.SemaphoreType.DMA((SLOTS,)),
        ],
        out_shape=[
            jax.ShapeDtypeStruct((rows, columns), jnp.float32),
            jax.ShapeDtypeStruct((1, share), jnp.float32),
        ],
        compiler_params=pltpu.CompilerParams(vmem_limit_bytes=28 * MIB),
        cost_estimate=pl.CostEstimate(
            flops=2 * rows * depth * columns,
            bytes_accessed=rows * depth * 2 + rows * columns * 4,
            transcendentals=0,
        ),
    )(
        lax.axis_index("aux").astype(jnp.int32)[None],
        *[in_hbm(piece) for piece in early],
        *[in_vmem(piece) for piece in steps[-1]],
        *[in_vmem(both) for both in dressed],
        *traces,
    )
    return slopes, collision.reshape(share)


def local(pair_green_block, cholesky_factors, green_one, screening):
    rows, columns = pair_green_block.shape
    vectors = cholesky_factors.shape[1]
    norb = green_one.shape[0]
    orb_count = columns // norb
    aux_size = lax.axis_size("aux")
    me = lax.axis_index("aux")
    length = rows // PIECES

    green, green_one = load(pair_green_block, green_one)
    trace_weights = lax.dynamic_slice_in_dim(
        green_one, me * orb_count, orb_count, 1
    ).T.reshape(1, columns)
    weights = screening[:, None]
    zeros = jnp.zeros((vectors, columns), jnp.float32)

    dressed, traced = [], []

    def finish(step, total):
        both, trace = sum_and_dress(step, total, weights, green_one, trace_weights)
        dressed.append(both)
        traced.append(trace)

    held = [cut(cholesky_factors, i * length, length) for i in range(PIECES)]
    finish(0, project(cholesky_factors, green, 0, zeros))
    steps = []
    for step in range(1, aux_size):
        total, pieces = zeros, []
        for i in range(PIECES):
            after = (dressed[-1], traced[-1]) if i == 0 else (total,)
            place = in_hbm if step < aux_size - 1 else in_vmem
            piece = gate(shifted(held[i], "aux", 1), place, *after)
            pieces.append(piece)
            first = i * length
            if step < aux_size - 1:
                total = project(piece, green, first, total)
            else:
                total = total + project_plain(piece, green[first : first + length])
        held = pieces
        steps.append(pieces)
        finish(step, total)

    trace = jnp.concatenate(traced, axis=0)
    traces = [trace] + [exchanged(trace, "aux", bits) for bits in range(1, aux_size)]
    return slope(cholesky_factors, steps, dressed, traces)


def solution(mesh):
    placed = (P("rows", "aux"), P("rows", "aux"), P(), P())
    return jax.shard_map(
        local,
        mesh=mesh,
        in_specs=placed,
        out_specs=(P("rows", "aux"), P(("rows", "aux"))),
        check_vma=False,
    )
```

```python
import functools

import jax
import jax.numpy as jnp
from jax import lax
from jax.experimental import pallas as pl
from jax.experimental.pallas import tpu as pltpu
from jax.sharding import PartitionSpec as P

HIGHEST = lax.Precision.HIGHEST
PIECES = 2
MIB = 1024 * 1024
FREE = pl.CostEstimate(flops=0, bytes_accessed=0, transcendentals=0)
ANYWHERE = pl.BlockSpec(memory_space=pl.ANY)
IN_VMEM = pl.BlockSpec(memory_space=pltpu.VMEM)


vmem_shape = pltpu.VMEM


def in_vmem(block):
    return pltpu.with_memory_space_constraint(block, pltpu.VMEM)


def in_hbm(block):
    return pltpu.with_memory_space_constraint(block, pltpu.HBM)


def shifted(block, axis, shift):
    count = lax.axis_size(axis)
    return lax.ppermute(block, axis, [(i, (i + shift) % count) for i in range(count)])


def exchanged(block, axis, bit):
    count = lax.axis_size(axis)
    return lax.ppermute(block, axis, [(i, i ^ bit) for i in range(count)])


def gate_body(*refs):
    del refs


def gate(block, place, *after):
    return pl.pallas_call(
        gate_body,
        out_shape=jax.ShapeDtypeStruct(block.shape, block.dtype),
        in_specs=[ANYWHERE] * (1 + len(after)),
        out_specs=ANYWHERE,
        input_output_aliases={0: 0},
        compiler_params=pltpu.CompilerParams(vmem_limit_bytes=2 * MIB),
        cost_estimate=FREE,
    )(place(block), *after)


def load_body(count, *refs):
    arrays, copies, semaphores = refs[:count], refs[count : 2 * count], refs[-1]
    moves = [
        pltpu.make_async_copy(array, copy, semaphores.at[i])
        for i, (array, copy) in enumerate(zip(arrays, copies))
    ]
    for move in moves:
        move.start()
    for move in moves:
        move.wait()


def load(*arrays):
    return pl.pallas_call(
        functools.partial(load_body, len(arrays)),
        out_shape=[vmem_shape(array.shape, array.dtype) for array in arrays],
        in_specs=[pl.BlockSpec(memory_space=pltpu.HBM)] * len(arrays),
        out_specs=[IN_VMEM] * len(arrays),
        scratch_shapes=[pltpu.SemaphoreType.DMA((len(arrays),))],
        compiler_params=pltpu.CompilerParams(vmem_limit_bytes=2 * MIB),
        cost_estimate=FREE,
    )(*[in_hbm(array) for array in arrays])


def cut_body(first, array_ref, piece_ref, semaphore):
    move = pltpu.make_async_copy(
        array_ref.at[pl.ds(first, piece_ref.shape[0]), :], piece_ref, semaphore
    )
    move.start()
    move.wait()


def cut(array, first, length):
    return pl.pallas_call(
        functools.partial(cut_body, first),
        out_shape=vmem_shape((length,) + array.shape[1:], array.dtype),
        in_specs=[pl.BlockSpec(memory_space=pltpu.HBM)],
        out_specs=IN_VMEM,
        scratch_shapes=[pltpu.SemaphoreType.DMA],
        compiler_params=pltpu.CompilerParams(vmem_limit_bytes=2 * MIB),
        cost_estimate=FREE,
    )(in_hbm(array))


def project_body(first, block, piece_ref, green_ref, acc_ref, total_ref):
    total_ref[...] = acc_ref[...]

    @pl.loop(0, piece_ref.shape[0] // block)
    def _(i):
        at = pl.multiple_of(i * block, block)
        total_ref[...] += lax.dot_general(
            piece_ref[pl.ds(at, block), :],
            green_ref[pl.ds(first + at, block), :],
            (((0,), (0,)), ((), ())),
            preferred_element_type=jnp.float32,
        )


def project(piece, green, first, so_far):
    length, vectors = piece.shape
    columns = green.shape[1]
    return pl.pallas_call(
        functools.partial(project_body, first, min(length, 1024)),
        out_shape=jax.ShapeDtypeStruct((vectors, columns), jnp.float32),
        in_specs=[IN_VMEM] * 3,
        out_specs=IN_VMEM,
        compiler_params=pltpu.CompilerParams(vmem_limit_bytes=6 * MIB),
        cost_estimate=FREE,
    )(piece, green, so_far)


def project_plain(piece, green_rows):
    return lax.dot_general(
        piece, green_rows, (((0,), (0,)), ((), ())), preferred_element_type=jnp.float32
    )


def add_up(arrays):
    while len(arrays) > 1:
        arrays = [arrays[i] + arrays[i + 1] for i in range(0, len(arrays), 2)]
    return arrays[0]


def add_body(*refs):
    refs[-1][...] = add_up([ref[...] for ref in refs[:-1]])


def add(*arrays):
    return pl.pallas_call(
        add_body,
        out_shape=jax.ShapeDtypeStruct(arrays[0].shape, arrays[0].dtype),
        compiler_params=pltpu.CompilerParams(vmem_limit_bytes=4 * MIB),
        cost_estimate=FREE,
    )(*[in_vmem(array) for array in arrays])


def dress_body(step, *refs):
    summand_refs, (weights_ref, green_ref, dressed_ref) = refs[:-3], refs[-3:]
    half = dressed_ref.shape[0]
    norb = green_ref.shape[0]
    aux_size = lax.axis_size("aux")
    owner = lax.rem(lax.axis_index("aux") - step + aux_size, aux_size)
    upper = lax.rem(lax.axis_index("rows"), 2)
    weights = weights_ref[pl.ds((owner * 2 + upper) * half, half), :]
    total = add_up([ref[...] for ref in summand_refs])
    green = green_ref[...]
    for first in range(0, total.shape[1], norb):
        mixed = jnp.dot(
            total[:, first : first + norb],
            green,
            precision=HIGHEST,
            preferred_element_type=jnp.float32,
        )
        dressed_ref[:, first : first + norb] = (mixed * weights).astype(jnp.bfloat16)


def dress(step, summands, weights, green_one):
    return pl.pallas_call(
        functools.partial(dress_body, step),
        out_shape=jax.ShapeDtypeStruct(summands[0].shape, jnp.bfloat16),
        compiler_params=pltpu.CompilerParams(vmem_limit_bytes=6 * MIB),
        cost_estimate=FREE,
    )(*[in_vmem(summand) for summand in summands], weights, in_vmem(green_one))


def join_body(mine_ref, other_ref, trace_ref, dressed_ref, traced_ref):
    half = mine_ref.shape[0]
    upper = lax.rem(lax.axis_index("rows"), 2)
    dressed_ref[pl.ds(pl.multiple_of(upper * half, half), half), :] = mine_ref[...]
    dressed_ref[pl.ds(pl.multiple_of((1 - upper) * half, half), half), :] = other_ref[...]
    row = trace_ref[...]
    high = row.astype(jnp.bfloat16).astype(jnp.float32)
    middle = (row - high).astype(jnp.bfloat16).astype(jnp.float32)
    parts = jnp.concatenate(
        [row - high - middle, middle, high, jnp.zeros((5, row.shape[1]), jnp.float32)], axis=0
    )
    traced = lax.dot_general(
        parts.astype(jnp.bfloat16),
        dressed_ref[...],
        (((1,), (1,)), ((), ())),
        preferred_element_type=jnp.float32,
    )
    traced_ref[...] = jnp.sum(traced, axis=0, keepdims=True)


def join(mine, other, trace_weights):
    half, columns = mine.shape
    return pl.pallas_call(
        join_body,
        out_shape=[
            jax.ShapeDtypeStruct((2 * half, columns), jnp.bfloat16),
            jax.ShapeDtypeStruct((1, 2 * half), jnp.float32),
        ],
        compiler_params=pltpu.CompilerParams(vmem_limit_bytes=6 * MIB),
        cost_estimate=FREE,
    )(in_vmem(mine), in_vmem(other), trace_weights)


def sum_and_dress(step, projection, weights, green_one, trace_weights):
    count = lax.axis_size("rows")
    half = projection.shape[0] // 2
    upper = lax.rem(lax.axis_index("rows"), 2) == 1
    low, high = projection[:half], projection[half:]
    summands = [
        jnp.where(upper, high, low),
        exchanged(jnp.where(upper, low, high), "rows", 1),
    ]
    bits = [1 << b for b in range(1, count.bit_length() - 1)]
    while bits:
        total = add(*summands)
        partners = [bits[0]] if len(bits) == 1 else [bits[0], bits[1], bits[0] ^ bits[1]]
        summands = [total] + [exchanged(total, "rows", partner) for partner in partners]
        bits = bits[2:]
    mine = dress(step, summands, weights, green_one)
    return join(mine, exchanged(mine, "rows", 1), trace_weights)


SLOTS = 3
PARTS = 2


def slope_early_body(pieces, *refs):
    slope_ref, factors_ref, came = refs[-3:]
    shards, rows = factors_ref.shape[:2]
    factor_refs, dressed_refs = refs[: 1 + (shards - 1) * pieces], refs[-3 - shards : -3]
    steps, length = came.shape[0], rows // pieces
    block = rows // steps

    def arrivals(at):
        first = at * block
        sources = [factor_refs[0].at[pl.ds(first, block), :]] + [
            factor_refs[1 + s * pieces + first // length].at[pl.ds(first % length, block), :]
            for s in range(shards - 1)
        ]
        return [
            pltpu.make_async_copy(
                source, factors_ref.at[s, pl.ds(first, block), :], came.at[at, s]
            )
            for s, source in enumerate(sources)
        ]

    for at in range(steps):
        for copy in arrivals(at):
            copy.start()
    dressed = jnp.concatenate([ref[...] for ref in dressed_refs], axis=0)
    for at in range(steps):
        for copy in arrivals(at):
            copy.wait()
        here = pl.ds(at * block, block)
        basis = jnp.concatenate([factors_ref[s, here, :] for s in range(shards)], axis=1)
        slope_ref[here, :] = jnp.dot(basis, dressed, preferred_element_type=jnp.float32)


def slope_early(factors, pieces, dressed):
    rows, vectors = factors[0].shape
    columns = dressed[0].shape[1]
    block = min(rows // pieces, 1024)
    return pl.pallas_call(
        functools.partial(slope_early_body, pieces),
        in_specs=[pl.BlockSpec(memory_space=pltpu.HBM)] * len(factors) + [IN_VMEM] * len(dressed),
        out_specs=IN_VMEM,
        out_shape=vmem_shape((rows, columns), jnp.float32),
        scratch_shapes=[
            pltpu.VMEM((len(dressed), rows, vectors), jnp.bfloat16),
            pltpu.SemaphoreType.DMA((rows // block, len(dressed))),
        ],
        compiler_params=pltpu.CompilerParams(vmem_limit_bytes=14 * MIB),
        cost_estimate=FREE,
    )(*[in_hbm(piece) for piece in factors], *[in_vmem(both) for both in dressed])


def slope_body(pieces, *refs):
    slope_ref, collision_ref, share_ref, held_ref, came, gone = refs[-6:]
    shards = share_ref.shape[0] + 1
    count = 1 + (shards - 2) * pieces
    factor_refs, last_refs = refs[:count], refs[count : count + pieces]
    early_ref, dressed_ref = refs[count + pieces : count + pieces + 2]
    trace_refs = refs[count + pieces + 2 : -6]
    rows, share, block = early_ref.shape[0], share_ref.shape[1], held_ref.shape[1]
    steps, length = rows // block, rows // pieces
    per_piece = length // share
    part = block // PARTS
    me = lax.axis_index("aux")

    def departures(at):
        return [
            pltpu.make_async_copy(
                held_ref.at[at % SLOTS, pl.ds(i * part, part), :],
                slope_ref.at[pl.ds(at * block + i * part, part), :],
                gone.at[at % SLOTS, i],
            )
            for i in range(PARTS)
        ]

    def arrivals(i):
        there = pl.ds(pl.multiple_of(me * share, share), share)
        here = pl.ds(pl.multiple_of((me - i * per_piece) * share, share), share)
        sources = [factor_refs[0].at[there, :]] + [
            factor_refs[1 + s * pieces + i].at[here, :] for s in range(shards - 2)
        ]
        return [
            pltpu.make_async_copy(source, share_ref.at[s], came.at[s])
            for s, source in enumerate(sources)
        ]

    for i in range(pieces):

        @pl.when(me // per_piece == i)
        def _():
            for copy in arrivals(i):
                copy.start()

    dressed = dressed_ref[...]
    for at in range(steps):
        if at >= SLOTS:
            for copy in departures(at - SLOTS):
                copy.wait()
        first = at * block
        held_ref[at % SLOTS] = early_ref[pl.ds(first, block), :] + jnp.dot(
            last_refs[first // length][pl.ds(first % length, block), :],
            dressed,
            preferred_element_type=jnp.float32,
        )
        for copy in departures(at):
            copy.start()

    trace = trace_refs[0][...]
    for shift in range(1, shards):
        other = trace_refs[shift][...]
        trace = trace + jnp.concatenate([other[shards - shift :], other[: shards - shift]], axis=0)
    row = jnp.concatenate([trace[s : s + 1] for s in range(shards)], axis=1)
    high = row.astype(jnp.bfloat16).astype(jnp.float32)
    middle = (row - high).astype(jnp.bfloat16).astype(jnp.float32)
    low = row - high - middle
    thirds = jnp.concatenate(
        [low, middle, high, jnp.zeros((5, row.shape[1]), jnp.float32)], axis=0
    ).astype(jnp.bfloat16)
    for i in range(pieces):

        @pl.when(me // per_piece == i)
        def _():
            for copy in arrivals(i):
                copy.wait()
            here = pl.ds(pl.multiple_of((me - i * per_piece) * share, share), share)
            basis = jnp.concatenate(
                [share_ref[s] for s in range(shards - 1)] + [last_refs[i][here, :]], axis=1
            )
            parts = lax.dot_general(
                thirds, basis, (((1,), (1,)), ((), ())), preferred_element_type=jnp.float32
            )
            collision_ref[...] = jnp.sum(parts, axis=0, keepdims=True)

    for at in range(max(steps - SLOTS, 0), steps):
        for copy in departures(at):
            copy.wait()


def slope(factors, last, early, dressed, traces):
    pieces, shards = len(last), len(traces)
    rows, columns = early.shape
    vectors = dressed.shape[0]
    share = rows // shards
    block = min(rows // pieces, 1024)
    far = pl.BlockSpec(memory_space=pltpu.HBM)
    slopes, collision = pl.pallas_call(
        functools.partial(slope_body, pieces),
        in_specs=[far] * len(factors) + [IN_VMEM] * (pieces + 2 + shards),
        out_specs=[far, IN_VMEM],
        scratch_shapes=[
            pltpu.VMEM((shards - 1, share, vectors), jnp.bfloat16),
            pltpu.VMEM((SLOTS, block, columns), jnp.float32),
            pltpu.SemaphoreType.DMA((shards - 1,)),
            pltpu.SemaphoreType.DMA((SLOTS, PARTS)),
        ],
        out_shape=[
            jax.ShapeDtypeStruct((rows, columns), jnp.float32),
            jax.ShapeDtypeStruct((1, share), jnp.float32),
        ],
        compiler_params=pltpu.CompilerParams(vmem_limit_bytes=20 * MIB),
        cost_estimate=pl.CostEstimate(
            flops=2 * rows * vectors * columns,
            bytes_accessed=rows * columns * 4,
            transcendentals=0,
        ),
    )(
        *[in_hbm(piece) for piece in factors],
        *[in_vmem(piece) for piece in last],
        in_vmem(early),
        in_vmem(dressed),
        *traces,
    )
    return slopes, collision.reshape(share)


def local(pair_green_block, cholesky_factors, green_one, screening):
    rows, columns = pair_green_block.shape
    vectors = cholesky_factors.shape[1]
    norb = green_one.shape[0]
    orb_count = columns // norb
    aux_size = lax.axis_size("aux")
    me = lax.axis_index("aux")
    length = rows // PIECES

    green, green_one = load(pair_green_block, green_one)
    trace_weights = lax.dynamic_slice_in_dim(
        green_one, me * orb_count, orb_count, 1
    ).T.reshape(1, columns)
    weights = screening[:, None]
    zeros = jnp.zeros((vectors, columns), jnp.float32)

    dressed, traced = [], []

    def finish(step, total):
        both, trace = sum_and_dress(step, total, weights, green_one, trace_weights)
        dressed.append(both)
        traced.append(trace)

    held = [cut(cholesky_factors, i * length, length) for i in range(PIECES)]
    finish(0, project(cholesky_factors, green, 0, zeros))
    steps = []
    for step in range(1, aux_size):
        total, pieces = zeros, []
        for i in range(PIECES):
            after = (dressed[-1], traced[-1]) if i == 0 else (total,)
            if step == aux_size - 1 and i == PIECES - 1:
                factors = [cholesky_factors] + [one for pair in steps for one in pair]
                early = slope_early(factors, PIECES, dressed)
                after += (early,)
            place = in_hbm if step < aux_size - 1 else in_vmem
            piece = gate(shifted(held[i], "aux", 1), place, *after)
            pieces.append(piece)
            first = i * length
            if step < aux_size - 1:
                total = project(piece, green, first, total)
            else:
                total = total + project_plain(piece, green[first : first + length])
        held = pieces
        steps.append(pieces)
        finish(step, total)

    trace = jnp.concatenate(traced, axis=0)
    traces = [trace] + [shifted(trace, "aux", shift) for shift in range(1, aux_size)]
    return slope(factors, steps[-1], early, dressed[-1], traces)


def solution(mesh):
    placed = (P("rows", "aux"), P("rows", "aux"), P(), P())
    return jax.shard_map(
        local,
        mesh=mesh,
        in_specs=placed,
        out_specs=(P("rows", "aux"), P(("rows", "aux"))),
        check_vma=False,
    )
```

```python
import functools

import jax
import jax.numpy as jnp
from jax import lax
from jax.experimental import pallas as pl
from jax.experimental.pallas import tpu as pltpu
from jax.sharding import PartitionSpec as P

HIGHEST = lax.Precision.HIGHEST
PIECES = 2
MIB = 1024 * 1024
FREE = pl.CostEstimate(flops=0, bytes_accessed=0, transcendentals=0)
ANYWHERE = pl.BlockSpec(memory_space=pl.ANY)
IN_VMEM = pl.BlockSpec(memory_space=pltpu.VMEM)


vmem_shape = pltpu.VMEM


def in_vmem(block):
    return pltpu.with_memory_space_constraint(block, pltpu.VMEM)


def in_hbm(block):
    return pltpu.with_memory_space_constraint(block, pltpu.HBM)


def shifted(block, axis, shift):
    count = lax.axis_size(axis)
    return lax.ppermute(block, axis, [(i, (i + shift) % count) for i in range(count)])


def exchanged(block, axis, bit):
    count = lax.axis_size(axis)
    return lax.ppermute(block, axis, [(i, i ^ bit) for i in range(count)])


def gather_traces(trace):
    rows, count = lax.axis_size("rows"), lax.axis_size("aux")
    pairs = []
    for first in range(1, count, 2):
        shifts = [first, min(first + 1, count - 1)]
        came = lax.ppermute(
            trace,
            ("rows", "aux"),
            [
                (row * count + i, row * count + (i + shifts[row % 2]) % count)
                for row in range(rows)
                for i in range(count)
            ],
        )
        pairs.append([came] if shifts[0] == shifts[1] else [came, exchanged(came, "rows", 1)])
    return [trace] + [array for pair in pairs for array in pair]


def gate_body(*refs):
    del refs


def gate(block, place, *after):
    return pl.pallas_call(
        gate_body,
        out_shape=jax.ShapeDtypeStruct(block.shape, block.dtype),
        in_specs=[ANYWHERE] * (1 + len(after)),
        out_specs=ANYWHERE,
        input_output_aliases={0: 0},
        compiler_params=pltpu.CompilerParams(vmem_limit_bytes=2 * MIB),
        cost_estimate=FREE,
    )(place(block), *after)


def load_body(count, *refs):
    arrays, copies, semaphores = refs[:count], refs[count : 2 * count], refs[-1]
    moves = [
        pltpu.make_async_copy(array, copy, semaphores.at[i])
        for i, (array, copy) in enumerate(zip(arrays, copies))
    ]
    for move in moves:
        move.start()
    for move in moves:
        move.wait()


def load(*arrays):
    return pl.pallas_call(
        functools.partial(load_body, len(arrays)),
        out_shape=[vmem_shape(array.shape, array.dtype) for array in arrays],
        in_specs=[pl.BlockSpec(memory_space=pltpu.HBM)] * len(arrays),
        out_specs=[IN_VMEM] * len(arrays),
        scratch_shapes=[pltpu.SemaphoreType.DMA((len(arrays),))],
        compiler_params=pltpu.CompilerParams(vmem_limit_bytes=2 * MIB),
        cost_estimate=FREE,
    )(*[in_hbm(array) for array in arrays])


def project_body(first, block, piece_ref, green_ref, acc_ref, total_ref):
    total_ref[...] = acc_ref[...]

    @pl.loop(0, piece_ref.shape[0] // block)
    def _(i):
        at = pl.multiple_of(i * block, block)
        total_ref[...] += lax.dot_general(
            piece_ref[pl.ds(at, block), :],
            green_ref[pl.ds(first + at, block), :],
            (((0,), (0,)), ((), ())),
            preferred_element_type=jnp.float32,
        )


def project(piece, green, first, so_far):
    length, vectors = piece.shape
    columns = green.shape[1]
    return pl.pallas_call(
        functools.partial(project_body, first, min(length, 1024)),
        out_shape=jax.ShapeDtypeStruct((vectors, columns), jnp.float32),
        in_specs=[IN_VMEM] * 3,
        out_specs=IN_VMEM,
        compiler_params=pltpu.CompilerParams(vmem_limit_bytes=6 * MIB),
        cost_estimate=FREE,
    )(piece, green, so_far)


def project_plain(piece, green_rows):
    return lax.dot_general(
        piece, green_rows, (((0,), (0,)), ((), ())), preferred_element_type=jnp.float32
    )


def add_up(arrays):
    while len(arrays) > 1:
        arrays = [arrays[i] + arrays[i + 1] for i in range(0, len(arrays), 2)]
    return arrays[0]


def add_body(*refs):
    refs[-1][...] = add_up([ref[...] for ref in refs[:-1]])


def add(*arrays):
    return pl.pallas_call(
        add_body,
        out_shape=jax.ShapeDtypeStruct(arrays[0].shape, arrays[0].dtype),
        compiler_params=pltpu.CompilerParams(vmem_limit_bytes=4 * MIB),
        cost_estimate=FREE,
    )(*[in_vmem(array) for array in arrays])


def dress_body(step, *refs):
    summand_refs, (weights_ref, green_ref, dressed_ref) = refs[:-3], refs[-3:]
    half = dressed_ref.shape[0]
    norb = green_ref.shape[0]
    aux_size = lax.axis_size("aux")
    owner = lax.rem(lax.axis_index("aux") - step + aux_size, aux_size)
    upper = lax.rem(lax.axis_index("rows"), 2)
    weights = weights_ref[pl.ds((owner * 2 + upper) * half, half), :]
    total = add_up([ref[...] for ref in summand_refs])
    green = green_ref[...]
    for first in range(0, total.shape[1], norb):
        mixed = jnp.dot(
            total[:, first : first + norb],
            green,
            precision=HIGHEST,
            preferred_element_type=jnp.float32,
        )
        dressed_ref[:, first : first + norb] = (mixed * weights).astype(jnp.bfloat16)


def dress(step, summands, weights, green_one):
    return pl.pallas_call(
        functools.partial(dress_body, step),
        out_shape=jax.ShapeDtypeStruct(summands[0].shape, jnp.bfloat16),
        compiler_params=pltpu.CompilerParams(vmem_limit_bytes=6 * MIB),
        cost_estimate=FREE,
    )(*[in_vmem(summand) for summand in summands], weights, in_vmem(green_one))


def join_body(mine_ref, other_ref, trace_ref, dressed_ref, traced_ref):
    half = mine_ref.shape[0]
    upper = lax.rem(lax.axis_index("rows"), 2)
    dressed_ref[pl.ds(pl.multiple_of(upper * half, half), half), :] = mine_ref[...]
    dressed_ref[pl.ds(pl.multiple_of((1 - upper) * half, half), half), :] = other_ref[...]
    row = trace_ref[...]
    high = row.astype(jnp.bfloat16).astype(jnp.float32)
    middle = (row - high).astype(jnp.bfloat16).astype(jnp.float32)
    parts = jnp.concatenate(
        [row - high - middle, middle, high, jnp.zeros((5, row.shape[1]), jnp.float32)], axis=0
    )
    traced = lax.dot_general(
        parts.astype(jnp.bfloat16),
        dressed_ref[...],
        (((1,), (1,)), ((), ())),
        preferred_element_type=jnp.float32,
    )
    traced_ref[...] = jnp.sum(traced, axis=0, keepdims=True)


def join(mine, other, trace_weights):
    half, columns = mine.shape
    return pl.pallas_call(
        join_body,
        out_shape=[
            jax.ShapeDtypeStruct((2 * half, columns), jnp.bfloat16),
            jax.ShapeDtypeStruct((1, 2 * half), jnp.float32),
        ],
        compiler_params=pltpu.CompilerParams(vmem_limit_bytes=6 * MIB),
        cost_estimate=FREE,
    )(in_vmem(mine), in_vmem(other), trace_weights)


def sum_and_dress(step, projection, weights, green_one, trace_weights):
    count = lax.axis_size("rows")
    half = projection.shape[0] // 2
    upper = lax.rem(lax.axis_index("rows"), 2) == 1
    low, high = projection[:half], projection[half:]
    summands = [
        jnp.where(upper, high, low),
        exchanged(jnp.where(upper, low, high), "rows", 1),
    ]
    bits = [1 << b for b in range(1, count.bit_length() - 1)]
    while bits:
        total = add(*summands)
        partners = [bits[0]] if len(bits) == 1 else [bits[0], bits[1], bits[0] ^ bits[1]]
        summands = [total] + [exchanged(total, "rows", partner) for partner in partners]
        bits = bits[2:]
    mine = dress(step, summands, weights, green_one)
    return join(mine, exchanged(mine, "rows", 1), trace_weights)


SLOTS = 3
PARTS = 2


def slope_early_body(pieces, *refs):
    slope_ref, factors_ref, came = refs[-3:]
    shards, rows = factors_ref.shape[:2]
    factor_refs, dressed_refs = refs[: 1 + (shards - 1) * pieces], refs[-3 - shards : -3]
    steps, length = came.shape[0], rows // pieces
    block = rows // steps

    def arrivals(at):
        first = at * block
        sources = [factor_refs[0].at[pl.ds(first, block), :]] + [
            factor_refs[1 + s * pieces + first // length].at[pl.ds(first % length, block), :]
            for s in range(shards - 1)
        ]
        return [
            pltpu.make_async_copy(
                source, factors_ref.at[s, pl.ds(first, block), :], came.at[at, s]
            )
            for s, source in enumerate(sources)
        ]

    for at in range(steps):
        for copy in arrivals(at):
            copy.start()
    dressed = jnp.concatenate([ref[...] for ref in dressed_refs], axis=0)
    for at in range(steps):
        for copy in arrivals(at):
            copy.wait()
        here = pl.ds(at * block, block)
        basis = jnp.concatenate([factors_ref[s, here, :] for s in range(shards)], axis=1)
        slope_ref[here, :] = jnp.dot(basis, dressed, preferred_element_type=jnp.float32)


def slope_early(factors, pieces, dressed):
    rows, vectors = factors[0].shape
    columns = dressed[0].shape[1]
    block = min(rows // pieces, 1024)
    return pl.pallas_call(
        functools.partial(slope_early_body, pieces),
        in_specs=[pl.BlockSpec(memory_space=pltpu.HBM)] * len(factors) + [IN_VMEM] * len(dressed),
        out_specs=IN_VMEM,
        out_shape=vmem_shape((rows, columns), jnp.float32),
        scratch_shapes=[
            pltpu.VMEM((len(dressed), rows, vectors), jnp.bfloat16),
            pltpu.SemaphoreType.DMA((rows // block, len(dressed))),
        ],
        compiler_params=pltpu.CompilerParams(vmem_limit_bytes=14 * MIB),
        cost_estimate=FREE,
    )(*[in_hbm(piece) for piece in factors], *[in_vmem(both) for both in dressed])


def slope_body(pieces, *refs):
    slope_ref, collision_ref, share_ref, held_ref, came, gone = refs[-6:]
    shards = share_ref.shape[0] + 1
    count = 1 + (shards - 2) * pieces
    factor_refs, last_refs = refs[:count], refs[count : count + pieces]
    early_ref, dressed_ref = refs[count + pieces : count + pieces + 2]
    trace_refs = refs[count + pieces + 2 : -6]
    rows, share, block = early_ref.shape[0], share_ref.shape[1], held_ref.shape[1]
    steps, length = rows // block, rows // pieces
    per_piece = length // share
    part = block // PARTS
    me = lax.axis_index("aux")

    def departures(at):
        return [
            pltpu.make_async_copy(
                held_ref.at[at % SLOTS, pl.ds(i * part, part), :],
                slope_ref.at[pl.ds(at * block + i * part, part), :],
                gone.at[at % SLOTS, i],
            )
            for i in range(PARTS)
        ]

    def arrivals(i):
        there = pl.ds(pl.multiple_of(me * share, share), share)
        here = pl.ds(pl.multiple_of((me - i * per_piece) * share, share), share)
        sources = [factor_refs[0].at[there, :]] + [
            factor_refs[1 + s * pieces + i].at[here, :] for s in range(shards - 2)
        ]
        return [
            pltpu.make_async_copy(source, share_ref.at[s], came.at[s])
            for s, source in enumerate(sources)
        ]

    for i in range(pieces):

        @pl.when(me // per_piece == i)
        def _():
            for copy in arrivals(i):
                copy.start()

    dressed = dressed_ref[...]
    for at in range(steps):
        if at >= SLOTS:
            for copy in departures(at - SLOTS):
                copy.wait()
        first = at * block
        held_ref[at % SLOTS] = early_ref[pl.ds(first, block), :] + jnp.dot(
            last_refs[first // length][pl.ds(first % length, block), :],
            dressed,
            preferred_element_type=jnp.float32,
        )
        for copy in departures(at):
            copy.start()

    odd = lax.rem(lax.axis_index("rows"), 2) == 1
    trace = trace_refs[0][...]
    for shift in range(1, shards):
        theirs = trace_refs[shift][...]
        pair = (shift - 1) // 2 * 2 + 1
        if pair + 1 < shards:
            theirs = jnp.where(odd == (shift > pair), trace_refs[pair][...], trace_refs[pair + 1][...])
        trace = trace + jnp.concatenate([theirs[shards - shift :], theirs[: shards - shift]], axis=0)
    row = jnp.concatenate([trace[s : s + 1] for s in range(shards)], axis=1)
    high = row.astype(jnp.bfloat16).astype(jnp.float32)
    middle = (row - high).astype(jnp.bfloat16).astype(jnp.float32)
    low = row - high - middle
    thirds = jnp.concatenate(
        [low, middle, high, jnp.zeros((5, row.shape[1]), jnp.float32)], axis=0
    ).astype(jnp.bfloat16)
    for i in range(pieces):

        @pl.when(me // per_piece == i)
        def _():
            for copy in arrivals(i):
                copy.wait()
            here = pl.ds(pl.multiple_of((me - i * per_piece) * share, share), share)
            basis = jnp.concatenate(
                [share_ref[s] for s in range(shards - 1)] + [last_refs[i][here, :]], axis=1
            )
            parts = lax.dot_general(
                thirds, basis, (((1,), (1,)), ((), ())), preferred_element_type=jnp.float32
            )
            collision_ref[...] = jnp.sum(parts, axis=0, keepdims=True)

    for at in range(max(steps - SLOTS, 0), steps):
        for copy in departures(at):
            copy.wait()


def slope(factors, last, early, dressed, traces):
    pieces, shards = len(last), len(traces)
    rows, columns = early.shape
    vectors = dressed.shape[0]
    share = rows // shards
    block = min(rows // pieces, 1024)
    far = pl.BlockSpec(memory_space=pltpu.HBM)
    slopes, collision = pl.pallas_call(
        functools.partial(slope_body, pieces),
        in_specs=[far] * len(factors) + [IN_VMEM] * (pieces + 2 + shards),
        out_specs=[far, IN_VMEM],
        scratch_shapes=[
            pltpu.VMEM((shards - 1, share, vectors), jnp.bfloat16),
            pltpu.VMEM((SLOTS, block, columns), jnp.float32),
            pltpu.SemaphoreType.DMA((shards - 1,)),
            pltpu.SemaphoreType.DMA((SLOTS, PARTS)),
        ],
        out_shape=[
            jax.ShapeDtypeStruct((rows, columns), jnp.float32),
            jax.ShapeDtypeStruct((1, share), jnp.float32),
        ],
        compiler_params=pltpu.CompilerParams(vmem_limit_bytes=20 * MIB),
        cost_estimate=pl.CostEstimate(
            flops=2 * rows * vectors * columns,
            bytes_accessed=rows * columns * 4,
            transcendentals=0,
        ),
    )(
        *[in_hbm(piece) for piece in factors],
        *[in_vmem(piece) for piece in last],
        in_vmem(early),
        in_vmem(dressed),
        *traces,
    )
    return slopes, collision.reshape(share)


def local(pair_green_block, cholesky_factors, green_one, screening):
    rows, columns = pair_green_block.shape
    vectors = cholesky_factors.shape[1]
    norb = green_one.shape[0]
    orb_count = columns // norb
    aux_size = lax.axis_size("aux")
    me = lax.axis_index("aux")
    length = rows // PIECES

    green, green_one = load(pair_green_block, green_one)
    trace_weights = lax.dynamic_slice_in_dim(
        green_one, me * orb_count, orb_count, 1
    ).T.reshape(1, columns)
    weights = screening[:, None]
    zeros = jnp.zeros((vectors, columns), jnp.float32)

    dressed, traced = [], []

    def finish(step, total):
        both, trace = sum_and_dress(step, total, weights, green_one, trace_weights)
        dressed.append(both)
        traced.append(trace)

    held = [
        gate(
            lax.slice_in_dim(cholesky_factors, i * length, (i + 1) * length, axis=0), in_vmem
        )
        for i in range(PIECES)
    ]
    finish(0, project(cholesky_factors, green, 0, zeros))
    steps = []
    for step in range(1, aux_size):
        total, pieces = zeros, []
        for i in range(PIECES):
            after = (dressed[-1], traced[-1]) if i == 0 else (total,)
            if step == aux_size - 1 and i == PIECES - 1:
                factors = [cholesky_factors] + [one for pair in steps for one in pair]
                early = slope_early(factors, PIECES, dressed)
                after += (early,)
            place = in_hbm if step < aux_size - 1 else in_vmem
            piece = gate(shifted(held[i], "aux", 1), place, *after)
            pieces.append(piece)
            first = i * length
            if step < aux_size - 1:
                total = project(piece, green, first, total)
            else:
                total = total + project_plain(piece, green[first : first + length])
        held = pieces
        steps.append(pieces)
        finish(step, total)

    trace = jnp.concatenate(traced, axis=0)
    traces = gather_traces(trace)
    return slope(factors, steps[-1], early, dressed[-1], traces)


def solution(mesh):
    placed = (P("rows", "aux"), P("rows", "aux"), P(), P())
    return jax.shard_map(
        local,
        mesh=mesh,
        in_specs=placed,
        out_specs=(P("rows", "aux"), P(("rows", "aux"))),
        check_vma=False,
    )
```

```python
import functools

import jax
import jax.numpy as jnp
from jax import lax
from jax.experimental import pallas as pl
from jax.experimental.pallas import tpu as pltpu
from jax.sharding import PartitionSpec as P

HIGHEST = lax.Precision.HIGHEST
PIECES = 2
MIB = 1024 * 1024
FREE = pl.CostEstimate(flops=0, bytes_accessed=0, transcendentals=0)
ANYWHERE = pl.BlockSpec(memory_space=pl.ANY)
IN_VMEM = pl.BlockSpec(memory_space=pltpu.VMEM)


vmem_shape = pltpu.VMEM


def in_vmem(block):
    return pltpu.with_memory_space_constraint(block, pltpu.VMEM)


def in_hbm(block):
    return pltpu.with_memory_space_constraint(block, pltpu.HBM)


def shifted(block, axis, shift):
    count = lax.axis_size(axis)
    return lax.ppermute(block, axis, [(i, (i + shift) % count) for i in range(count)])


def exchanged(block, axis, bit):
    count = lax.axis_size(axis)
    return lax.ppermute(block, axis, [(i, i ^ bit) for i in range(count)])


def gather_traces(trace):
    rows, count = lax.axis_size("rows"), lax.axis_size("aux")
    pairs = []
    for first in range(1, count, 2):
        shifts = [first, min(first + 1, count - 1)]
        came = lax.ppermute(
            trace,
            ("rows", "aux"),
            [
                (row * count + i, row * count + (i + shifts[row % 2]) % count)
                for row in range(rows)
                for i in range(count)
            ],
        )
        pairs.append([came] if shifts[0] == shifts[1] else [came, exchanged(came, "rows", 1)])
    return [trace] + [array for pair in pairs for array in pair]


def gate_body(*refs):
    del refs


def gate(block, place, *after):
    return pl.pallas_call(
        gate_body,
        out_shape=jax.ShapeDtypeStruct(block.shape, block.dtype),
        in_specs=[ANYWHERE] * (1 + len(after)),
        out_specs=ANYWHERE,
        input_output_aliases={0: 0},
        compiler_params=pltpu.CompilerParams(vmem_limit_bytes=2 * MIB),
        cost_estimate=FREE,
    )(place(block), *after)


def load_body(count, *refs):
    arrays, copies, semaphores = refs[:count], refs[count : 2 * count], refs[-1]
    moves = [
        pltpu.make_async_copy(array, copy, semaphores.at[i])
        for i, (array, copy) in enumerate(zip(arrays, copies))
    ]
    for move in moves:
        move.start()
    for move in moves:
        move.wait()


def load(*arrays):
    return pl.pallas_call(
        functools.partial(load_body, len(arrays)),
        out_shape=[vmem_shape(array.shape, array.dtype) for array in arrays],
        in_specs=[pl.BlockSpec(memory_space=pltpu.HBM)] * len(arrays),
        out_specs=[IN_VMEM] * len(arrays),
        scratch_shapes=[pltpu.SemaphoreType.DMA((len(arrays),))],
        compiler_params=pltpu.CompilerParams(vmem_limit_bytes=2 * MIB),
        cost_estimate=FREE,
    )(*[in_hbm(array) for array in arrays])


def cut_body(first, array_ref, piece_ref, semaphore):
    move = pltpu.make_async_copy(
        array_ref.at[pl.ds(first, piece_ref.shape[0]), :], piece_ref, semaphore
    )
    move.start()
    move.wait()


def cut(array, first, length):
    return pl.pallas_call(
        functools.partial(cut_body, first),
        out_shape=vmem_shape((length,) + array.shape[1:], array.dtype),
        in_specs=[pl.BlockSpec(memory_space=pltpu.HBM)],
        out_specs=IN_VMEM,
        scratch_shapes=[pltpu.SemaphoreType.DMA],
        compiler_params=pltpu.CompilerParams(vmem_limit_bytes=2 * MIB),
        cost_estimate=FREE,
    )(in_hbm(array))


def project_body(first, block, piece_ref, green_ref, acc_ref, total_ref):
    total_ref[...] = acc_ref[...]

    @pl.loop(0, piece_ref.shape[0] // block)
    def _(i):
        at = pl.multiple_of(i * block, block)
        total_ref[...] += lax.dot_general(
            piece_ref[pl.ds(at, block), :],
            green_ref[pl.ds(first + at, block), :],
            (((0,), (0,)), ((), ())),
            preferred_element_type=jnp.float32,
        )


def project(piece, green, first, so_far):
    length, vectors = piece.shape
    columns = green.shape[1]
    return pl.pallas_call(
        functools.partial(project_body, first, min(length, 1024)),
        out_shape=jax.ShapeDtypeStruct((vectors, columns), jnp.float32),
        in_specs=[IN_VMEM] * 3,
        out_specs=IN_VMEM,
        compiler_params=pltpu.CompilerParams(vmem_limit_bytes=6 * MIB),
        cost_estimate=FREE,
    )(piece, green, so_far)


def project_plain(piece, green_rows):
    return lax.dot_general(
        piece, green_rows, (((0,), (0,)), ((), ())), preferred_element_type=jnp.float32
    )


def add_up(arrays):
    while len(arrays) > 1:
        arrays = [arrays[i] + arrays[i + 1] for i in range(0, len(arrays), 2)]
    return arrays[0]


def add_body(*refs):
    refs[-1][...] = add_up([ref[...] for ref in refs[:-1]])


def add(*arrays):
    return pl.pallas_call(
        add_body,
        out_shape=jax.ShapeDtypeStruct(arrays[0].shape, arrays[0].dtype),
        compiler_params=pltpu.CompilerParams(vmem_limit_bytes=4 * MIB),
        cost_estimate=FREE,
    )(*[in_vmem(array) for array in arrays])


def dress_body(step, *refs):
    summand_refs, (weights_ref, green_ref, dressed_ref) = refs[:-3], refs[-3:]
    half = dressed_ref.shape[0]
    norb = green_ref.shape[0]
    aux_size = lax.axis_size("aux")
    owner = lax.rem(lax.axis_index("aux") - step + aux_size, aux_size)
    upper = lax.rem(lax.axis_index("rows"), 2)
    weights = weights_ref[pl.ds((owner * 2 + upper) * half, half), :]
    total = add_up([ref[...] for ref in summand_refs])
    green = green_ref[...]
    for first in range(0, total.shape[1], norb):
        mixed = jnp.dot(
            total[:, first : first + norb],
            green,
            precision=HIGHEST,
            preferred_element_type=jnp.float32,
        )
        dressed_ref[:, first : first + norb] = (mixed * weights).astype(jnp.bfloat16)


def dress(step, summands, weights, green_one):
    return pl.pallas_call(
        functools.partial(dress_body, step),
        out_shape=jax.ShapeDtypeStruct(summands[0].shape, jnp.bfloat16),
        compiler_params=pltpu.CompilerParams(vmem_limit_bytes=6 * MIB),
        cost_estimate=FREE,
    )(*[in_vmem(summand) for summand in summands], weights, in_vmem(green_one))


def join_body(mine_ref, other_ref, trace_ref, dressed_ref, traced_ref):
    half = mine_ref.shape[0]
    upper = lax.rem(lax.axis_index("rows"), 2)
    dressed_ref[pl.ds(pl.multiple_of(upper * half, half), half), :] = mine_ref[...]
    dressed_ref[pl.ds(pl.multiple_of((1 - upper) * half, half), half), :] = other_ref[...]
    row = trace_ref[...]
    high = row.astype(jnp.bfloat16).astype(jnp.float32)
    middle = (row - high).astype(jnp.bfloat16).astype(jnp.float32)
    parts = jnp.concatenate(
        [row - high - middle, middle, high, jnp.zeros((5, row.shape[1]), jnp.float32)], axis=0
    )
    traced = lax.dot_general(
        parts.astype(jnp.bfloat16),
        dressed_ref[...],
        (((1,), (1,)), ((), ())),
        preferred_element_type=jnp.float32,
    )
    traced_ref[...] = jnp.sum(traced, axis=0, keepdims=True)


def join(mine, other, trace_weights):
    half, columns = mine.shape
    return pl.pallas_call(
        join_body,
        out_shape=[
            jax.ShapeDtypeStruct((2 * half, columns), jnp.bfloat16),
            jax.ShapeDtypeStruct((1, 2 * half), jnp.float32),
        ],
        compiler_params=pltpu.CompilerParams(vmem_limit_bytes=6 * MIB),
        cost_estimate=FREE,
    )(in_vmem(mine), in_vmem(other), trace_weights)


def sum_and_dress(step, projection, weights, green_one, trace_weights):
    count = lax.axis_size("rows")
    half = projection.shape[0] // 2
    upper = lax.rem(lax.axis_index("rows"), 2) == 1
    low, high = projection[:half], projection[half:]
    summands = [
        jnp.where(upper, high, low),
        exchanged(jnp.where(upper, low, high), "rows", 1),
    ]
    bits = [1 << b for b in range(1, count.bit_length() - 1)]
    while bits:
        total = add(*summands)
        partners = [bits[0]] if len(bits) == 1 else [bits[0], bits[1], bits[0] ^ bits[1]]
        summands = [total] + [exchanged(total, "rows", partner) for partner in partners]
        bits = bits[2:]
    mine = dress(step, summands, weights, green_one)
    return join(mine, exchanged(mine, "rows", 1), trace_weights)


SLOTS = 3
PARTS = 2


def slope_early_body(pieces, *refs):
    slope_ref, factors_ref, came = refs[-3:]
    shards, rows = factors_ref.shape[:2]
    factor_refs, dressed_refs = refs[: 1 + (shards - 1) * pieces], refs[-3 - shards : -3]
    steps, length = came.shape[0], rows // pieces
    block = rows // steps

    def arrivals(at):
        first = at * block
        sources = [factor_refs[0].at[pl.ds(first, block), :]] + [
            factor_refs[1 + s * pieces + first // length].at[pl.ds(first % length, block), :]
            for s in range(shards - 1)
        ]
        return [
            pltpu.make_async_copy(
                source, factors_ref.at[s, pl.ds(first, block), :], came.at[at, s]
            )
            for s, source in enumerate(sources)
        ]

    for at in range(steps):
        for copy in arrivals(at):
            copy.start()
    dressed = jnp.concatenate([ref[...] for ref in dressed_refs], axis=0)
    for at in range(steps):
        for copy in arrivals(at):
            copy.wait()
        here = pl.ds(at * block, block)
        basis = jnp.concatenate([factors_ref[s, here, :] for s in range(shards)], axis=1)
        slope_ref[here, :] = jnp.dot(basis, dressed, preferred_element_type=jnp.float32)


def slope_early(factors, pieces, dressed):
    rows, vectors = factors[0].shape
    columns = dressed[0].shape[1]
    block = min(rows // pieces, 1024)
    return pl.pallas_call(
        functools.partial(slope_early_body, pieces),
        in_specs=[pl.BlockSpec(memory_space=pltpu.HBM)] * len(factors) + [IN_VMEM] * len(dressed),
        out_specs=IN_VMEM,
        out_shape=vmem_shape((rows, columns), jnp.float32),
        scratch_shapes=[
            pltpu.VMEM((len(dressed), rows, vectors), jnp.bfloat16),
            pltpu.SemaphoreType.DMA((rows // block, len(dressed))),
        ],
        compiler_params=pltpu.CompilerParams(vmem_limit_bytes=14 * MIB),
        cost_estimate=FREE,
    )(*[in_hbm(piece) for piece in factors], *[in_vmem(both) for both in dressed])


def slope_body(pieces, *refs):
    slope_ref, collision_ref, share_ref, held_ref, came, gone = refs[-6:]
    shards = share_ref.shape[0] + 1
    count = 1 + (shards - 2) * pieces
    factor_refs, last_refs = refs[:count], refs[count : count + pieces]
    early_ref, dressed_ref = refs[count + pieces : count + pieces + 2]
    trace_refs = refs[count + pieces + 2 : -6]
    rows, share, block = early_ref.shape[0], share_ref.shape[1], held_ref.shape[1]
    steps, length = rows // block, rows // pieces
    per_piece = length // share
    part = block // PARTS
    me = lax.axis_index("aux")

    def departures(at):
        return [
            pltpu.make_async_copy(
                held_ref.at[at % SLOTS, pl.ds(i * part, part), :],
                slope_ref.at[pl.ds(at * block + i * part, part), :],
                gone.at[at % SLOTS, i],
            )
            for i in range(PARTS)
        ]

    def arrivals(i):
        there = pl.ds(pl.multiple_of(me * share, share), share)
        here = pl.ds(pl.multiple_of((me - i * per_piece) * share, share), share)
        sources = [factor_refs[0].at[there, :]] + [
            factor_refs[1 + s * pieces + i].at[here, :] for s in range(shards - 2)
        ]
        return [
            pltpu.make_async_copy(source, share_ref.at[s], came.at[s])
            for s, source in enumerate(sources)
        ]

    for i in range(pieces):

        @pl.when(me // per_piece == i)
        def _():
            for copy in arrivals(i):
                copy.start()

    dressed = dressed_ref[...]
    for at in range(steps):
        if at >= SLOTS:
            for copy in departures(at - SLOTS):
                copy.wait()
        first = at * block
        held_ref[at % SLOTS] = early_ref[pl.ds(first, block), :] + jnp.dot(
            last_refs[first // length][pl.ds(first % length, block), :],
            dressed,
            preferred_element_type=jnp.float32,
        )
        for copy in departures(at):
            copy.start()

    odd = lax.rem(lax.axis_index("rows"), 2) == 1
    trace = trace_refs[0][...]
    for shift in range(1, shards):
        theirs = trace_refs[shift][...]
        pair = (shift - 1) // 2 * 2 + 1
        if pair + 1 < shards:
            theirs = jnp.where(odd == (shift > pair), trace_refs[pair][...], trace_refs[pair + 1][...])
        trace = trace + jnp.concatenate([theirs[shards - shift :], theirs[: shards - shift]], axis=0)
    row = jnp.concatenate([trace[s : s + 1] for s in range(shards)], axis=1)
    high = row.astype(jnp.bfloat16).astype(jnp.float32)
    middle = (row - high).astype(jnp.bfloat16).astype(jnp.float32)
    low = row - high - middle
    thirds = jnp.concatenate(
        [low, middle, high, jnp.zeros((5, row.shape[1]), jnp.float32)], axis=0
    ).astype(jnp.bfloat16)
    for i in range(pieces):

        @pl.when(me // per_piece == i)
        def _():
            for copy in arrivals(i):
                copy.wait()
            here = pl.ds(pl.multiple_of((me - i * per_piece) * share, share), share)
            basis = jnp.concatenate(
                [share_ref[s] for s in range(shards - 1)] + [last_refs[i][here, :]], axis=1
            )
            parts = lax.dot_general(
                thirds, basis, (((1,), (1,)), ((), ())), preferred_element_type=jnp.float32
            )
            collision_ref[...] = jnp.sum(parts, axis=0, keepdims=True)

    for at in range(max(steps - SLOTS, 0), steps):
        for copy in departures(at):
            copy.wait()


def slope(factors, last, early, dressed, traces):
    pieces, shards = len(last), len(traces)
    rows, columns = early.shape
    vectors = dressed.shape[0]
    share = rows // shards
    block = min(rows // pieces, 1024)
    far = pl.BlockSpec(memory_space=pltpu.HBM)
    slopes, collision = pl.pallas_call(
        functools.partial(slope_body, pieces),
        in_specs=[far] * len(factors) + [IN_VMEM] * (pieces + 2 + shards),
        out_specs=[far, IN_VMEM],
        scratch_shapes=[
            pltpu.VMEM((shards - 1, share, vectors), jnp.bfloat16),
            pltpu.VMEM((SLOTS, block, columns), jnp.float32),
            pltpu.SemaphoreType.DMA((shards - 1,)),
            pltpu.SemaphoreType.DMA((SLOTS, PARTS)),
        ],
        out_shape=[
            jax.ShapeDtypeStruct((rows, columns), jnp.float32),
            jax.ShapeDtypeStruct((1, share), jnp.float32),
        ],
        compiler_params=pltpu.CompilerParams(vmem_limit_bytes=20 * MIB),
        cost_estimate=pl.CostEstimate(
            flops=2 * rows * vectors * columns,
            bytes_accessed=rows * columns * 4,
            transcendentals=0,
        ),
    )(
        *[in_hbm(piece) for piece in factors],
        *[in_vmem(piece) for piece in last],
        in_vmem(early),
        in_vmem(dressed),
        *traces,
    )
    return slopes, collision.reshape(share)


def local(pair_green_block, cholesky_factors, green_one, screening):
    rows, columns = pair_green_block.shape
    vectors = cholesky_factors.shape[1]
    norb = green_one.shape[0]
    orb_count = columns // norb
    aux_size = lax.axis_size("aux")
    me = lax.axis_index("aux")
    length = rows // PIECES

    green, green_one = load(pair_green_block, green_one)
    trace_weights = lax.dynamic_slice_in_dim(
        green_one, me * orb_count, orb_count, 1
    ).T.reshape(1, columns)
    weights = screening[:, None]
    zeros = jnp.zeros((vectors, columns), jnp.float32)

    dressed, traced = [], []

    def finish(step, total):
        both, trace = sum_and_dress(step, total, weights, green_one, trace_weights)
        dressed.append(both)
        traced.append(trace)

    held = [cut(cholesky_factors, i * length, length) for i in range(PIECES)]
    finish(0, project(cholesky_factors, green, 0, zeros))
    steps = []
    for step in range(1, aux_size):
        total, pieces = zeros, []
        for i in range(PIECES):
            after = (dressed[-1], traced[-1]) if i == 0 else (total,)
            if step == aux_size - 1 and i == PIECES - 1:
                factors = [cholesky_factors] + [one for pair in steps for one in pair]
                early = slope_early(factors, PIECES, dressed)
                after += (early,)
            place = in_hbm if step < aux_size - 1 else in_vmem
            piece = gate(shifted(held[i], "aux", 1), place, *after)
            pieces.append(piece)
            first = i * length
            if step < aux_size - 1:
                total = project(piece, green, first, total)
            else:
                total = total + project_plain(piece, green[first : first + length])
        held = pieces
        steps.append(pieces)
        finish(step, total)

    trace = jnp.concatenate(traced, axis=0)
    traces = gather_traces(trace)
    return slope(factors, steps[-1], early, dressed[-1], traces)


def solution(mesh):
    placed = (P("rows", "aux"), P("rows", "aux"), P(), P())
    return jax.shard_map(
        local,
        mesh=mesh,
        in_specs=placed,
        out_specs=(P("rows", "aux"), P(("rows", "aux"))),
        check_vma=False,
    )
```

```python
import functools

import jax
import jax.numpy as jnp
from jax import lax
from jax.experimental import pallas as pl
from jax.experimental.pallas import tpu as pltpu
from jax.sharding import PartitionSpec as P

HIGHEST = lax.Precision.HIGHEST
PIECES = 2
MIB = 1024 * 1024
FREE = pl.CostEstimate(flops=0, bytes_accessed=0, transcendentals=0)
ANYWHERE = pl.BlockSpec(memory_space=pl.ANY)
IN_VMEM = pl.BlockSpec(memory_space=pltpu.VMEM)


vmem_shape = pltpu.VMEM


def in_vmem(block):
    return pltpu.with_memory_space_constraint(block, pltpu.VMEM)


def in_hbm(block):
    return pltpu.with_memory_space_constraint(block, pltpu.HBM)


def shifted(block, axis, shift):
    count = lax.axis_size(axis)
    return lax.ppermute(block, axis, [(i, (i + shift) % count) for i in range(count)])


def exchanged(block, axis, bit):
    count = lax.axis_size(axis)
    return lax.ppermute(block, axis, [(i, i ^ bit) for i in range(count)])


def gather_traces(trace):
    rows, count = lax.axis_size("rows"), lax.axis_size("aux")
    pairs = []
    for first in range(1, count, 2):
        shifts = [first, min(first + 1, count - 1)]
        came = lax.ppermute(
            trace,
            ("rows", "aux"),
            [
                (row * count + i, row * count + (i + shifts[row % 2]) % count)
                for row in range(rows)
                for i in range(count)
            ],
        )
        pairs.append([came] if shifts[0] == shifts[1] else [came, exchanged(came, "rows", 1)])
    return [trace] + [array for pair in pairs for array in pair]


def gate_body(*refs):
    del refs


def gate(block, place, *after):
    return pl.pallas_call(
        gate_body,
        out_shape=jax.ShapeDtypeStruct(block.shape, block.dtype),
        in_specs=[ANYWHERE] * (1 + len(after)),
        out_specs=ANYWHERE,
        input_output_aliases={0: 0},
        compiler_params=pltpu.CompilerParams(vmem_limit_bytes=2 * MIB),
        cost_estimate=FREE,
    )(place(block), *after)


def load_body(count, *refs):
    arrays, copies, semaphores = refs[:count], refs[count : 2 * count], refs[-1]
    moves = [
        pltpu.make_async_copy(array, copy, semaphores.at[i])
        for i, (array, copy) in enumerate(zip(arrays, copies))
    ]
    for move in moves:
        move.start()
    for move in moves:
        move.wait()


def load(*arrays):
    return pl.pallas_call(
        functools.partial(load_body, len(arrays)),
        out_shape=[vmem_shape(array.shape, array.dtype) for array in arrays],
        in_specs=[pl.BlockSpec(memory_space=pltpu.HBM)] * len(arrays),
        out_specs=[IN_VMEM] * len(arrays),
        scratch_shapes=[pltpu.SemaphoreType.DMA((len(arrays),))],
        compiler_params=pltpu.CompilerParams(vmem_limit_bytes=2 * MIB),
        cost_estimate=FREE,
    )(*[in_hbm(array) for array in arrays])


def cut_body(first, array_ref, piece_ref, semaphore):
    move = pltpu.make_async_copy(
        array_ref.at[pl.ds(first, piece_ref.shape[0]), :], piece_ref, semaphore
    )
    move.start()
    move.wait()


def cut(array, first, length):
    return pl.pallas_call(
        functools.partial(cut_body, first),
        out_shape=vmem_shape((length,) + array.shape[1:], array.dtype),
        in_specs=[pl.BlockSpec(memory_space=pltpu.HBM)],
        out_specs=IN_VMEM,
        scratch_shapes=[pltpu.SemaphoreType.DMA],
        compiler_params=pltpu.CompilerParams(vmem_limit_bytes=2 * MIB),
        cost_estimate=FREE,
    )(in_hbm(array))


def project_body(first, block, piece_ref, green_ref, acc_ref, total_ref):
    total_ref[...] = acc_ref[...]

    @pl.loop(0, piece_ref.shape[0] // block)
    def _(i):
        at = pl.multiple_of(i * block, block)
        total_ref[...] += lax.dot_general(
            piece_ref[pl.ds(at, block), :],
            green_ref[pl.ds(first + at, block), :],
            (((0,), (0,)), ((), ())),
            preferred_element_type=jnp.float32,
        )


def project(piece, green, first, so_far):
    length, vectors = piece.shape
    columns = green.shape[1]
    return pl.pallas_call(
        functools.partial(project_body, first, min(length, 1024)),
        out_shape=jax.ShapeDtypeStruct((vectors, columns), jnp.float32),
        in_specs=[IN_VMEM] * 3,
        out_specs=IN_VMEM,
        compiler_params=pltpu.CompilerParams(vmem_limit_bytes=6 * MIB),
        cost_estimate=FREE,
    )(piece, green, so_far)


def project_plain(piece, green_rows):
    return lax.dot_general(
        piece, green_rows, (((0,), (0,)), ((), ())), preferred_element_type=jnp.float32
    )


def add_up(arrays):
    while len(arrays) > 1:
        arrays = [arrays[i] + arrays[i + 1] for i in range(0, len(arrays), 2)]
    return arrays[0]


def add_body(*refs):
    refs[-1][...] = add_up([ref[...] for ref in refs[:-1]])


def add(*arrays):
    return pl.pallas_call(
        add_body,
        out_shape=jax.ShapeDtypeStruct(arrays[0].shape, arrays[0].dtype),
        compiler_params=pltpu.CompilerParams(vmem_limit_bytes=4 * MIB),
        cost_estimate=FREE,
    )(*[in_vmem(array) for array in arrays])


def dress_body(step, *refs):
    summand_refs, (weights_ref, green_ref, dressed_ref) = refs[:-3], refs[-3:]
    half = dressed_ref.shape[0]
    norb = green_ref.shape[0]
    aux_size = lax.axis_size("aux")
    owner = lax.rem(lax.axis_index("aux") - step + aux_size, aux_size)
    upper = lax.rem(lax.axis_index("rows"), 2)
    weights = weights_ref[pl.ds((owner * 2 + upper) * half, half), :]
    total = add_up([ref[...] for ref in summand_refs])
    green = green_ref[...]
    for first in range(0, total.shape[1], norb):
        mixed = jnp.dot(
            total[:, first : first + norb],
            green,
            precision=HIGHEST,
            preferred_element_type=jnp.float32,
        )
        dressed_ref[:, first : first + norb] = (mixed * weights).astype(jnp.bfloat16)


def dress(step, summands, weights, green_one):
    return pl.pallas_call(
        functools.partial(dress_body, step),
        out_shape=jax.ShapeDtypeStruct(summands[0].shape, jnp.bfloat16),
        compiler_params=pltpu.CompilerParams(vmem_limit_bytes=6 * MIB),
        cost_estimate=FREE,
    )(*[in_vmem(summand) for summand in summands], weights, in_vmem(green_one))


def join_body(mine_ref, other_ref, trace_ref, dressed_ref, traced_ref):
    half = mine_ref.shape[0]
    upper = lax.rem(lax.axis_index("rows"), 2)
    dressed_ref[pl.ds(pl.multiple_of(upper * half, half), half), :] = mine_ref[...]
    dressed_ref[pl.ds(pl.multiple_of((1 - upper) * half, half), half), :] = other_ref[...]
    row = trace_ref[...]
    high = row.astype(jnp.bfloat16).astype(jnp.float32)
    middle = (row - high).astype(jnp.bfloat16).astype(jnp.float32)
    parts = jnp.concatenate(
        [row - high - middle, middle, high, jnp.zeros((5, row.shape[1]), jnp.float32)], axis=0
    )
    traced = lax.dot_general(
        parts.astype(jnp.bfloat16),
        dressed_ref[...],
        (((1,), (1,)), ((), ())),
        preferred_element_type=jnp.float32,
    )
    traced_ref[...] = jnp.sum(traced, axis=0, keepdims=True)


def join(mine, other, trace_weights):
    half, columns = mine.shape
    return pl.pallas_call(
        join_body,
        out_shape=[
            jax.ShapeDtypeStruct((2 * half, columns), jnp.bfloat16),
            jax.ShapeDtypeStruct((1, 2 * half), jnp.float32),
        ],
        compiler_params=pltpu.CompilerParams(vmem_limit_bytes=6 * MIB),
        cost_estimate=FREE,
    )(in_vmem(mine), in_vmem(other), trace_weights)


def sum_and_dress(step, projection, weights, green_one, trace_weights):
    count = lax.axis_size("rows")
    half = projection.shape[0] // 2
    upper = lax.rem(lax.axis_index("rows"), 2) == 1
    low, high = projection[:half], projection[half:]
    summands = [
        jnp.where(upper, high, low),
        exchanged(jnp.where(upper, low, high), "rows", 1),
    ]
    bits = [1 << b for b in range(1, count.bit_length() - 1)]
    while bits:
        total = add(*summands)
        partners = [bits[0]] if len(bits) == 1 else [bits[0], bits[1], bits[0] ^ bits[1]]
        came = [exchanged(total, "rows", partner) for partner in partners[::-1]]
        summands = [total] + came[::-1]
        bits = bits[2:]
    mine = dress(step, summands, weights, green_one)
    return join(mine, exchanged(mine, "rows", 1), trace_weights)


SLOTS = 3
PARTS = 2


def slope_early_body(pieces, *refs):
    slope_ref, factors_ref, came = refs[-3:]
    shards, rows = factors_ref.shape[:2]
    factor_refs, dressed_refs = refs[: 1 + (shards - 1) * pieces], refs[-3 - shards : -3]
    steps, length = came.shape[0], rows // pieces
    block = rows // steps

    def arrivals(at):
        first = at * block
        sources = [factor_refs[0].at[pl.ds(first, block), :]] + [
            factor_refs[1 + s * pieces + first // length].at[pl.ds(first % length, block), :]
            for s in range(shards - 1)
        ]
        return [
            pltpu.make_async_copy(
                source, factors_ref.at[s, pl.ds(first, block), :], came.at[at, s]
            )
            for s, source in enumerate(sources)
        ]

    for at in range(steps):
        for copy in arrivals(at):
            copy.start()
    dressed = jnp.concatenate([ref[...] for ref in dressed_refs], axis=0)
    for at in range(steps):
        for copy in arrivals(at):
            copy.wait()
        here = pl.ds(at * block, block)
        basis = jnp.concatenate([factors_ref[s, here, :] for s in range(shards)], axis=1)
        slope_ref[here, :] = jnp.dot(basis, dressed, preferred_element_type=jnp.float32)


def slope_early(factors, pieces, dressed):
    rows, vectors = factors[0].shape
    columns = dressed[0].shape[1]
    block = min(rows // pieces, 1024)
    return pl.pallas_call(
        functools.partial(slope_early_body, pieces),
        in_specs=[pl.BlockSpec(memory_space=pltpu.HBM)] * len(factors) + [IN_VMEM] * len(dressed),
        out_specs=IN_VMEM,
        out_shape=vmem_shape((rows, columns), jnp.float32),
        scratch_shapes=[
            pltpu.VMEM((len(dressed), rows, vectors), jnp.bfloat16),
            pltpu.SemaphoreType.DMA((rows // block, len(dressed))),
        ],
        compiler_params=pltpu.CompilerParams(vmem_limit_bytes=14 * MIB),
        cost_estimate=FREE,
    )(*[in_hbm(piece) for piece in factors], *[in_vmem(both) for both in dressed])


def slope_body(pieces, *refs):
    slope_ref, collision_ref, share_ref, held_ref, came, gone = refs[-6:]
    shards = share_ref.shape[0] + 1
    count = 1 + (shards - 2) * pieces
    factor_refs, last_refs = refs[:count], refs[count : count + pieces]
    early_ref, dressed_ref = refs[count + pieces : count + pieces + 2]
    trace_refs = refs[count + pieces + 2 : -6]
    rows, share, block = early_ref.shape[0], share_ref.shape[1], held_ref.shape[1]
    steps, length = rows // block, rows // pieces
    per_piece = length // share
    part = block // PARTS
    me = lax.axis_index("aux")

    def departures(at):
        return [
            pltpu.make_async_copy(
                held_ref.at[at % SLOTS, pl.ds(i * part, part), :],
                slope_ref.at[pl.ds(at * block + i * part, part), :],
                gone.at[at % SLOTS, i],
            )
            for i in range(PARTS)
        ]

    def arrivals(i):
        there = pl.ds(pl.multiple_of(me * share, share), share)
        here = pl.ds(pl.multiple_of((me - i * per_piece) * share, share), share)
        sources = [factor_refs[0].at[there, :]] + [
            factor_refs[1 + s * pieces + i].at[here, :] for s in range(shards - 2)
        ]
        return [
            pltpu.make_async_copy(source, share_ref.at[s], came.at[s])
            for s, source in enumerate(sources)
        ]

    for i in range(pieces):

        @pl.when(me // per_piece == i)
        def _():
            for copy in arrivals(i):
                copy.start()

    dressed = dressed_ref[...]
    for at in range(steps):
        if at >= SLOTS:
            for copy in departures(at - SLOTS):
                copy.wait()
        first = at * block
        held_ref[at % SLOTS] = early_ref[pl.ds(first, block), :] + jnp.dot(
            last_refs[first // length][pl.ds(first % length, block), :],
            dressed,
            preferred_element_type=jnp.float32,
        )
        for copy in departures(at):
            copy.start()

    odd = lax.rem(lax.axis_index("rows"), 2) == 1
    trace = trace_refs[0][...]
    for shift in range(1, shards):
        theirs = trace_refs[shift][...]
        pair = (shift - 1) // 2 * 2 + 1
        if pair + 1 < shards:
            theirs = jnp.where(odd == (shift > pair), trace_refs[pair][...], trace_refs[pair + 1][...])
        trace = trace + jnp.concatenate([theirs[shards - shift :], theirs[: shards - shift]], axis=0)
    row = jnp.concatenate([trace[s : s + 1] for s in range(shards)], axis=1)
    high = row.astype(jnp.bfloat16).astype(jnp.float32)
    middle = (row - high).astype(jnp.bfloat16).astype(jnp.float32)
    low = row - high - middle
    thirds = jnp.concatenate(
        [low, middle, high, jnp.zeros((5, row.shape[1]), jnp.float32)], axis=0
    ).astype(jnp.bfloat16)
    for i in range(pieces):

        @pl.when(me // per_piece == i)
        def _():
            for copy in arrivals(i):
                copy.wait()
            here = pl.ds(pl.multiple_of((me - i * per_piece) * share, share), share)
            basis = jnp.concatenate(
                [share_ref[s] for s in range(shards - 1)] + [last_refs[i][here, :]], axis=1
            )
            parts = lax.dot_general(
                thirds, basis, (((1,), (1,)), ((), ())), preferred_element_type=jnp.float32
            )
            collision_ref[...] = jnp.sum(parts, axis=0, keepdims=True)

    for at in range(max(steps - SLOTS, 0), steps):
        for copy in departures(at):
            copy.wait()


def slope(factors, last, early, dressed, traces):
    pieces, shards = len(last), len(traces)
    rows, columns = early.shape
    vectors = dressed.shape[0]
    share = rows // shards
    block = min(rows // pieces, 1024)
    far = pl.BlockSpec(memory_space=pltpu.HBM)
    slopes, collision = pl.pallas_call(
        functools.partial(slope_body, pieces),
        in_specs=[far] * len(factors) + [IN_VMEM] * (pieces + 2 + shards),
        out_specs=[far, IN_VMEM],
        scratch_shapes=[
            pltpu.VMEM((shards - 1, share, vectors), jnp.bfloat16),
            pltpu.VMEM((SLOTS, block, columns), jnp.float32),
            pltpu.SemaphoreType.DMA((shards - 1,)),
            pltpu.SemaphoreType.DMA((SLOTS, PARTS)),
        ],
        out_shape=[
            jax.ShapeDtypeStruct((rows, columns), jnp.float32),
            jax.ShapeDtypeStruct((1, share), jnp.float32),
        ],
        compiler_params=pltpu.CompilerParams(vmem_limit_bytes=20 * MIB),
        cost_estimate=pl.CostEstimate(
            flops=2 * rows * vectors * columns,
            bytes_accessed=rows * columns * 4,
            transcendentals=0,
        ),
    )(
        *[in_hbm(piece) for piece in factors],
        *[in_vmem(piece) for piece in last],
        in_vmem(early),
        in_vmem(dressed),
        *traces,
    )
    return slopes, collision.reshape(share)


def local(pair_green_block, cholesky_factors, green_one, screening):
    rows, columns = pair_green_block.shape
    vectors = cholesky_factors.shape[1]
    norb = green_one.shape[0]
    orb_count = columns // norb
    aux_size = lax.axis_size("aux")
    me = lax.axis_index("aux")
    length = rows // PIECES

    green, green_one = load(pair_green_block, green_one)
    trace_weights = lax.dynamic_slice_in_dim(
        green_one, me * orb_count, orb_count, 1
    ).T.reshape(1, columns)
    weights = screening[:, None]
    zeros = jnp.zeros((vectors, columns), jnp.float32)

    dressed, traced = [], []

    def finish(step, total):
        both, trace = sum_and_dress(step, total, weights, green_one, trace_weights)
        dressed.append(both)
        traced.append(trace)

    held = [cut(cholesky_factors, i * length, length) for i in range(PIECES)]
    finish(0, project(cholesky_factors, green, 0, zeros))
    steps = []
    for step in range(1, aux_size):
        total, pieces = zeros, []
        for i in range(PIECES):
            after = (dressed[-1], traced[-1]) if i == 0 else (total,)
            if step == aux_size - 1 and i == PIECES - 1:
                factors = [cholesky_factors] + [one for pair in steps for one in pair]
                early = slope_early(factors, PIECES, dressed)
                after += (early,)
            place = in_hbm if step < aux_size - 1 else in_vmem
            piece = gate(shifted(held[i], "aux", 1), place, *after)
            pieces.append(piece)
            first = i * length
            if step < aux_size - 1:
                total = project(piece, green, first, total)
            else:
                total = total + project_plain(piece, green[first : first + length])
        held = pieces
        steps.append(pieces)
        finish(step, total)

    trace = jnp.concatenate(traced, axis=0)
    traces = gather_traces(trace)
    return slope(factors, steps[-1], early, dressed[-1], traces)


def solution(mesh):
    placed = (P("rows", "aux"), P("rows", "aux"), P(), P())
    return jax.shard_map(
        local,
        mesh=mesh,
        in_specs=placed,
        out_specs=(P("rows", "aux"), P(("rows", "aux"))),
        check_vma=False,
    )
```
